256 devices in a mesh: row: 16 (over x, y_hi, core), col: 16 (over z, y_lo).
Axes of the slice: x: 4, y: 4 (y_hi: 2, y_lo: 2; y = y_hi * 2 + y_lo), z: 8, core: 2. Of those that a mesh axis runs over, the one named last changes fastest.
Arguments:
- block_values: float32 [64, 16, 3, 128, 128], P('row', 'col'), may hold values from -1.5 to 1.5
- block_cols: int32 [64, 16, 3], P('row', 'col'), may hold values from 0 to 3
- result_cols: int32 [64, 16, 4], P('row', 'col'), may hold values from 0 to 3, each once within a row
Outputs:
- square_blocks: float32 [64, 16, 4, 128, 128], P('row', 'col')
The draws below stay inside these ranges and needn't reach their ends.
Inputs may be any that keep to these rules, and one draw needn't show every extreme that they name: `block_cols`: a stored block's column inside its run of 4 block columns; several stored blocks may share a column. For each block row i and each tile q, result_cols[i, q, :] is a permutation of 0 to 3, so each value appears once in every tile and 16 times over a whole block row.
All inputs are finite; a program needn't handle non-finite values.
Results may differ from the reference program's by a relative error of at most 0.0003.
Values sent between devices are 32-bit elements; how exact they have to be, the bound alone decides.
A program may use at most 192 MiB of HBM per device.

```python
import jax
import jax.numpy as jnp
from jax import lax

BS = 128
BR = 4
S = 3
SR = 4
NB = 64
N_ROW = 16
N_COL = 16


def place_ends(drawn, rng, least, largest):
    shape = drawn.shape
    index_at = [jax.random.randint(jax.random.fold_in(rng, axis), (), 0, shape[axis]) for axis in range(len(shape))]
    drawn = drawn.at[tuple(index_at)].set(least)
    longest = shape.index(max(shape))
    index_at[longest] = (index_at[longest] + 1) % shape[longest]
    return drawn.at[tuple(index_at)].set(largest)


def levels(key, dims, cuts, smallest, top_value):
    def one(axis_at, blocks):
        draws = jax.random.uniform(jax.random.fold_in(jax.random.fold_in(key, 6), axis_at), (blocks,), jnp.float32, smallest / len(cuts), top_value / len(cuts))
        return jnp.repeat(jnp.exp(draws), dims[axis_at] // blocks).reshape((-1,) + (1,) * (len(dims) - axis_at - 1))

    factor_of = one(*cuts[0])
    for cut in cuts[1:]:
        factor_of = factor_of * one(*cut)
    return factor_of


def noise(own_key, dims, spread, limit, split=(), dtype=jnp.bfloat16):
    values = jax.random.normal(own_key, dims, jnp.float32) * spread
    if len(split) > 0:
        values = levels(own_key, dims, split, -0.22, 0.18) * values
    return jnp.clip(values, min=-limit, max=limit).astype(dtype)


def setup_inputs(seed: int = 0) -> dict:
    keys = jax.random.split(jax.random.key(seed), 4)
    return {
        "block_values": noise(keys[0], (NB, N_ROW, S, BS, BS), 0.25, 1.5, ((0, 16), (1, 16)), jnp.float32),
        "block_cols": place_ends(jax.random.randint(keys[1], (NB, N_ROW, S), 0, BR), jax.random.fold_in(keys[1], 1), 0, BR - 1).astype(jnp.int32),
        "result_cols": jax.vmap(lambda own: jax.random.permutation(own, BR * N_ROW // N_COL))(jax.random.split(keys[2], NB * N_COL)).reshape((NB, N_COL, SR)).astype(jnp.int32),
    }


def reference(block_values, block_cols, result_cols):
    total_rows = block_values.shape[0]
    piece_ids = jnp.arange(N_ROW).astype(jnp.int32)
    global_cols = (piece_ids[None, :, None] * BR + block_cols.astype(jnp.int32)).reshape(total_rows, N_ROW * S)
    flat_values = block_values.reshape(total_rows, N_ROW * S, BS, BS)
    tile_ids = jnp.arange(N_COL).astype(jnp.int32)
    target_cols = (tile_ids[None, :, None] * (BR * N_ROW // N_COL) + result_cols.astype(jnp.int32)).reshape(total_rows, N_COL * SR)

    def one_row(row_index):
        left_blocks = flat_values[row_index]
        inner_rows = global_cols[row_index]
        right_blocks = flat_values[inner_rows]
        right_cols = global_cols[inner_rows]
        products = jnp.einsum("kxy,kmyz->kmxz", left_blocks, right_blocks, precision=lax.Precision.HIGHEST)
        matches = (right_cols[:, :, None] == target_cols[row_index][None, None, :]).astype(jnp.float32)
        return jnp.einsum("kmu,kmxz->uxz", matches, products, precision=lax.Precision.HIGHEST)

    result = lax.map(one_row, jnp.arange(total_rows).astype(jnp.int32))
    return result.reshape(total_rows, N_COL, SR, BS, BS)
```

```python
import functools

import jax
import jax.numpy as jnp
from jax import lax
from jax.experimental import pallas as pl
from jax.experimental.pallas import tpu as pltpu
from jax.sharding import PartitionSpec as P

MESH = pl.DeviceIdType.MESH
NX, NZ = 4, 8
ORDER = 128
STORED, SLOTS, ROWS = 3, 4, 4
BODY = STORED * ORDER
PIECE = BODY + 8
CUT = 192
RING = 7 * ROWS
STEPS = 35

PRODUCTS = (
    (9, 0, 0, 0),
    (15, 0, 0, 1),
    (16, 1, 0, 0),
    (17, 1, 0, 1),
    (21, 2, 0, 0),
    (22, 2, 0, 1),
    (23, 0, 1, 0),
    (24, 1, 1, 0),
    (25, 2, 1, 0),
    (28, 3, 0, 0),
    (29, 3, 0, 1),
    (30, 0, 1, 1),
    (31, 1, 1, 1),
    (32, 2, 1, 1),
    (33, 3, 1, 0),
    (34, 3, 1, 1),
)


def spread(piece, write):
    step = 32
    heads = [piece[BODY + s : BODY + s + 1, :] for s in range(STORED)]
    hits = [
        [jnp.broadcast_to(heads[s], (step, ORDER)) == float(k) for s in range(STORED)]
        for k in range(SLOTS)
    ]
    for r in range(0, ORDER, step):
        blocks = [piece[s * ORDER + r : s * ORDER + r + step, :] for s in range(STORED)]
        for k in range(SLOTS):
            total = jnp.where(hits[k][0], blocks[0], 0.0)
            for s in range(1, STORED):
                total = total + jnp.where(hits[k][s], blocks[s], 0.0)
            high = total.astype(jnp.bfloat16)
            low = (total - high.astype(jnp.float32)).astype(jnp.bfloat16)
            write(r, step, k, high, low)


def kernel(
    vals, bcols, rcols, out,
    abuf, bbuf, ad, bhi, blo, cacc, crecv, ostg,
    stage_sem, za_send, za_recv, y_send, y_recv, x_send, x_recv, s_send, s_recv, c_send, c_recv, o_sem,
):
    row, col = lax.axis_index("row"), lax.axis_index("col")
    x, yh, c = lax.div(row, 4), lax.rem(lax.div(row, 2), 2), lax.rem(row, 2)
    z, yl = lax.div(col, 2), lax.rem(col, 2)

    def at_row(x_, yh_, c_):
        return (x_ * 2 + yh_) * 2 + c_

    z_up, z_down = lax.rem(z + 1, NZ), lax.rem(z + NZ - 1, NZ)
    x_up, x_down = lax.rem(x + 1, NX), lax.rem(x + NX - 1, NX)
    sibling = (at_row(x, yh, 1 - c), col)
    partner = (row, z * 2 + 1 - yl)
    z_side = ((row, z_up * 2 + yl), (row, z_down * 2 + yl))
    alone = jnp.logical_and(yh == c, c == yl)

    for p in range(ROWS):
        pltpu.make_async_copy(
            vals.at[p], abuf.at[z, p, pl.ds(0, BODY)], stage_sem.at[p]
        ).start()

    barrier = pltpu.get_barrier_semaphore()

    def greet(device):
        pl.semaphore_signal(barrier, inc=1, device_id=device, device_id_type=MESH)

    greet(z_side[0])
    greet(z_side[1])
    greet((at_row(x_up, yh, c), col))
    greet((at_row(x_down, yh, c), col))
    greet(sibling)
    greet(partner)
    for k in range(2):
        @pl.when(jnp.logical_not(jnp.logical_and(alone, yh == k)))
        def _():
            greet((at_row(x, k, yh), z * 2 + c))
            greet((at_row(x, c, yl), z * 2 + k))

    for p in range(ROWS):
        head = [
            jnp.full((1, ORDER), bcols[p, 0, s].astype(jnp.float32)) for s in range(STORED)
        ]
        head = head + [jnp.zeros((8 - STORED, ORDER), jnp.float32)]
        abuf[z, p, BODY:PIECE, :] = jnp.concatenate(head, axis=0)
    for p in range(ROWS):
        pltpu.make_async_copy(
            vals.at[p], abuf.at[z, p, pl.ds(0, BODY)], stage_sem.at[p]
        ).wait()
    pl.semaphore_wait(barrier, jnp.where(alone, 8, 10))

    def z_copy(way, n, back):
        p, m = lax.div(n, 7), lax.rem(n, 7)
        far = lax.div(m, 2) + back
        source = lax.rem(z + (NZ - far if way == 0 else far), NZ)
        for parity in range(2):
            first = parity if way == 0 else 1 - parity
            rows = pl.ds(0, CUT) if first == 0 else pl.ds(CUT, PIECE - CUT)
            ref = abuf.at[source, p, rows]
            yield lax.rem(m, 2) == parity, pltpu.make_async_remote_copy(
                src_ref=ref,
                dst_ref=ref,
                send_sem=za_send.at[way, n],
                recv_sem=za_recv.at[way, n],
                device_id=z_side[way],
                device_id_type=MESH,
            )

    def z_start(way, n):
        for when, copy in z_copy(way, n, 0):
            pl.when(when)(copy.start)

    def z_arrive(way, n):
        for when, copy in z_copy(way, n, 1):
            pl.when(when)(copy.wait_recv)

    def z_sent(way, n):
        for when, copy in z_copy(way, n, 0):
            pl.when(when)(copy.wait_send)

    def turn(i):
        return 1 - 2 * lax.rem(c + lax.div(i, ROWS), 2)

    def along_x(steps):
        return lax.rem(x + steps + 2 * NX, NX)

    def x_copy(role, i):
        t = turn(i)
        source = along_x(-t) if role == 2 else x
        target = along_x(-t) if role == 1 else along_x(t)
        ref = bbuf.at[i, source * 2 + c]
        return pltpu.make_async_remote_copy(
            src_ref=ref,
            dst_ref=ref,
            send_sem=x_send.at[role, i],
            recv_sem=x_recv.at[role, i],
            device_id=(at_row(target, yh, c), col),
            device_id_type=MESH,
        )

    def x_source(role, i):
        t = turn(i)
        return (along_x(-t), along_x(t), along_x(2), x)[role]

    def x_arrive(role, i):
        ref = bbuf.at[i, x_source(role, i) * 2 + c]
        pltpu.make_async_remote_copy(
            src_ref=ref,
            dst_ref=ref,
            send_sem=x_send.at[role, i],
            recv_sem=x_recv.at[role, i],
            device_id=(at_row(x_up, yh, c), col),
            device_id_type=MESH,
        ).wait_recv()

    def s_copy(role, i):
        ref = bbuf.at[i, x_source(role, i) * 2 + c]
        return pltpu.make_async_remote_copy(
            src_ref=ref,
            dst_ref=ref,
            send_sem=s_send.at[role, i],
            recv_sem=s_recv.at[role, i],
            device_id=sibling,
            device_id_type=MESH,
        )

    def s_arrive(role, i):
        source = (x_source(1, i), x_source(0, i), along_x(2), x)[role]
        ref = bbuf.at[i, source * 2 + 1 - c]
        pltpu.make_async_remote_copy(
            src_ref=ref,
            dst_ref=ref,
            send_sem=s_send.at[role, i],
            recv_sem=s_recv.at[role, i],
            device_id=sibling,
            device_id_type=MESH,
        ).wait_recv()

    def y_copy(k, p):
        i = jnp.where(c == yl, ROWS, 0) + p
        return pltpu.make_async_remote_copy(
            src_ref=abuf.at[z, p],
            dst_ref=bbuf.at[i, x * 2 + yh],
            send_sem=y_send.at[k, p],
            recv_sem=y_recv.at[i],
            device_id=(at_row(x, k, yh), z * 2 + c),
            device_id_type=MESH,
        )

    def y_local(p):
        return pltpu.make_async_copy(
            abuf.at[z, p], bbuf.at[ROWS + p, x * 2 + yh], y_recv.at[ROWS + p]
        )

    def y_start():
        @pl.loop(0, ROWS)
        def _(p):
            for k in range(2):
                here = jnp.logical_and(alone, yh == k)
                pl.when(here)(lambda: y_local(p).start())
                pl.when(jnp.logical_not(here))(lambda: y_copy(k, p).start())

    def y_arrive(i):
        ref = bbuf.at[i, x * 2 + c]
        own = jnp.logical_and(alone, i >= ROWS)

        @pl.when(own)
        def _():
            y_local(lax.rem(i, ROWS)).wait()

        @pl.when(jnp.logical_not(own))
        def _():
            pltpu.make_async_remote_copy(
                src_ref=ref,
                dst_ref=ref,
                send_sem=y_send.at[0, 0],
                recv_sem=y_recv.at[i],
                device_id=sibling,
                device_id_type=MESH,
            ).wait_recv()

    def c_copy(p):
        return pltpu.make_async_remote_copy(
            src_ref=cacc.at[p],
            dst_ref=crecv.at[p],
            send_sem=c_send.at[p],
            recv_sem=c_recv.at[p],
            device_id=partner,
            device_id_type=MESH,
        )

    def spread_left(source, p):
        lanes = pl.multiple_of(source * 2 * ORDER, 2 * ORDER)

        def write(r, step, k, high, low):
            at = pl.ds(lanes + (k % 2) * ORDER, ORDER)
            ad[p * 2 + k // 2, r : r + step, at] = high
            ad[p * 2 + k // 2, ORDER + r : ORDER + r + step, at] = low

        spread(abuf.at[source, p], write)

    def spread_right(i, slot):
        base = pl.multiple_of(slot * 2 * ORDER + lax.rem(i, 2) * ORDER, ORDER)

        def write(r, step, k, high, low):
            rows = pl.ds(base + r, step)
            cols = pl.ds(k * ORDER, ORDER)
            bhi[lax.div(i, 2), rows, cols] = high
            blo[lax.div(i, 2), rows, cols] = low

        spread(bbuf.at[i, slot], write)

    def product(p, phase, half):
        left = ad.at[p * 2 + half]
        both = jnp.dot(left[...], bhi[phase * 2 + half], preferred_element_type=jnp.float32)
        rest = jnp.dot(left[0:ORDER, :], blo[phase * 2 + half], preferred_element_type=jnp.float32)
        total = both[0:ORDER] + (both[ORDER:] + rest)
        at = phase * ROWS + p
        cacc[at] = jnp.where(half == 0, 0.0, cacc[at]) + total

    for n in range(2):
        for way in range(2):
            z_start(way, jnp.int32(n))

    @pl.loop(0, STEPS)
    def _(n):
        p, m = lax.div(n, 7), lax.rem(n, 7)
        third = lax.rem(n, 3)

        @pl.when(n == jnp.where(c == yl, 4, 0))
        def _():
            y_start()

        @pl.when(n < RING)
        def _():
            for way in range(2):
                z_arrive(way, n)

                @pl.when(n + 2 < RING)
                def _():
                    z_start(way, n + 2)

        y_now = jnp.logical_or(n < ROWS, jnp.logical_and(n >= 2 * ROWS, n < 3 * ROWS))

        @pl.when(y_now)
        def _():
            i = jnp.where(n < ROWS, n, n - ROWS)
            y_arrive(i)
            x_copy(0, i).start()
            x_copy(1, i).start()
            s_copy(3, i).start()

        @pl.when(jnp.logical_and(third == 2, n <= 23))
        def _():
            i = lax.div(n, 3)
            x_arrive(0, i)
            x_copy(2, i).start()
            x_arrive(1, i)
            s_copy(0, i).start()
            s_copy(1, i).start()

        @pl.when(jnp.logical_and(third == 1, jnp.logical_and(n >= 4, n <= 25)))
        def _():
            i = lax.div(n, 3) - 1
            x_arrive(2, i)
            s_copy(2, i).start()

        near = jnp.logical_and(third == 0, jnp.logical_and(n >= 3, n <= 24))
        rest = jnp.logical_and(third == 2, jnp.logical_and(n >= 5, n <= 26))
        i_right = jnp.clip(lax.div(n, 3) - 1, 0, 2 * ROWS - 1)

        @pl.when(near)
        def _():
            s_arrive(0, i_right)
            s_arrive(1, i_right)

        @pl.when(rest)
        def _():
            s_arrive(2, i_right)
            s_arrive(3, i_right)

        @pl.when(jnp.logical_or(near, rest))
        def _():
            @pl.loop(0, 4)
            def _(k):
                away = lax.rem(k, 2) * 2 + jnp.where(near, 1, 0)
                spread_right(i_right, along_x(away) * 2 + lax.div(k, 2))

        @pl.when(n < RING)
        def _():
            far = jnp.where(m == 0, 0, lax.div(m + 2, 2))
            count = jnp.where(
                jnp.logical_or(m == 0, m == 6), 1, jnp.where(lax.rem(m, 2) == 1, 2, 0)
            )

            @pl.loop(0, count)
            def _(k):
                source = lax.rem(z + jnp.where(k == 0, far, NZ - far), NZ)
                spread_left(source, p)

        code = jnp.int32(0)
        for at, left_row, phase, half in PRODUCTS:
            code = code + jnp.where(n == at, 1 + left_row * 4 + phase * 2 + half, 0)

        @pl.when(code > 0)
        def _():
            unit = jnp.maximum(code - 1, 0)
            left_row, phase, half = lax.div(unit, 4), lax.rem(lax.div(unit, 2), 2), lax.rem(unit, 2)
            product(left_row, phase, half)

            @pl.when(jnp.logical_and(phase == 0, half == 1))
            def _():
                c_copy(left_row).start()

    @pl.loop(0, ROWS)
    def _(p):
        c_copy(p).wait_recv()
        for u in range(SLOTS):
            want = rcols[p, 0, u]
            for r in range(0, ORDER, 32):
                rows = slice(r, r + 32)
                block = jnp.zeros((32, ORDER), jnp.float32)
                for k in range(SLOTS):
                    cols = slice(k * ORDER, (k + 1) * ORDER)
                    both = cacc[ROWS + p, rows, cols] + crecv[p, rows, cols]
                    block = jnp.where(want == k, both, block)
                ostg[p, u, rows, :] = block
        pltpu.make_async_copy(ostg.at[p], out.at[p, 0], o_sem.at[p]).start()

    @pl.loop(0, RING)
    def _(n):
        for way in range(2):
            z_sent(way, n)

    @pl.loop(0, ROWS)
    def _(p):
        for k in range(2):
            pl.when(jnp.logical_not(jnp.logical_and(alone, yh == k)))(
                lambda: y_copy(k, p).wait_send()
            )
        c_copy(p).wait_send()

    @pl.loop(0, 2 * ROWS)
    def _(i):
        for role in range(3):
            x_copy(role, i).wait_send()
        for role in range(4):
            s_copy(role, i).wait_send()

    @pl.loop(0, ROWS)
    def _(p):
        pltpu.make_async_copy(ostg.at[p], out.at[p, 0], o_sem.at[p]).wait()


def on_device(block_values, block_cols, result_cols):
    vals = block_values.reshape(ROWS, BODY, ORDER)
    dma = pltpu.SemaphoreType.DMA
    return pl.pallas_call(
        kernel,
        out_shape=jax.ShapeDtypeStruct((ROWS, 1, SLOTS, ORDER, ORDER), jnp.float32),
        in_specs=[
            pl.BlockSpec(memory_space=pl.ANY),
            pl.BlockSpec(memory_space=pltpu.SMEM),
            pl.BlockSpec(memory_space=pltpu.SMEM),
        ],
        out_specs=pl.BlockSpec(memory_space=pl.ANY),
        scratch_shapes=[
            pltpu.VMEM((NZ, ROWS, PIECE, ORDER), jnp.float32),
            pltpu.VMEM((2 * ROWS, 2 * NX, PIECE, ORDER), jnp.float32),
            pltpu.VMEM((2 * ROWS, 2 * ORDER, NZ * 2 * ORDER), jnp.bfloat16),
            pltpu.VMEM((4, NZ * 2 * ORDER, SLOTS * ORDER), jnp.bfloat16),
            pltpu.VMEM((4, NZ * 2 * ORDER, SLOTS * ORDER), jnp.bfloat16),
            pltpu.VMEM((2 * ROWS, ORDER, SLOTS * ORDER), jnp.float32),
            pltpu.VMEM((ROWS, ORDER, SLOTS * ORDER), jnp.float32),
            pltpu.VMEM((ROWS, SLOTS, ORDER, ORDER), jnp.float32),
            dma((ROWS,)),
            dma((2, RING)),
            dma((2, RING)),
            dma((2, ROWS)),
            dma((2 * ROWS,)),
            dma((3, 2 * ROWS)),
            dma((3, 2 * ROWS)),
            dma((4, 2 * ROWS)),
            dma((4, 2 * ROWS)),
            dma((ROWS,)),
            dma((ROWS,)),
            dma((ROWS,)),
        ],
        compiler_params=pltpu.CompilerParams(
            collective_id=0, has_side_effects=True, vmem_limit_bytes=60 * 2**20
        ),
    )(vals, block_cols, result_cols)


def solution(mesh):
    return jax.shard_map(
        on_device,
        mesh=mesh,
        in_specs=(P("row", "col", None, None, None), P("row", "col", None), P("row", "col", None)),
        out_specs=P("row", "col", None, None, None),
        check_vma=False,
    )
```

```python
import functools

import jax
import jax.numpy as jnp
from jax import lax
from jax.experimental import pallas as pl
from jax.experimental.pallas import tpu as pltpu
from jax.sharding import PartitionSpec as P

MESH = pl.DeviceIdType.MESH
NX, NZ = 4, 8
ORDER = 128
STORED, SLOTS, ROWS = 3, 4, 4
BODY = STORED * ORDER
PIECE = BODY + 8
CUT = 192
CHAIN = 14
RING = 2 * CHAIN
PHASE = 3 * ROWS
STEPS = 35

PRODUCTS = (
    (10, 0, 0, 0),
    (15, 0, 0, 1),
    (16, 1, 0, 0),
    (17, 1, 0, 1),
    (19, 0, 1, 0),
    (20, 1, 1, 0),
    (23, 2, 0, 0),
    (24, 2, 0, 1),
    (25, 2, 1, 0),
    (28, 3, 0, 0),
    (29, 3, 0, 1),
    (30, 0, 1, 1),
    (31, 1, 1, 1),
    (32, 2, 1, 1),
    (33, 3, 1, 0),
    (34, 3, 1, 1),
)


def spread(piece, write):
    step = 32
    heads = [piece[BODY + s : BODY + s + 1, :] for s in range(STORED)]
    hits = [
        [jnp.broadcast_to(heads[s], (step, ORDER)) == float(k) for s in range(STORED)]
        for k in range(SLOTS)
    ]
    for r in range(0, ORDER, step):
        blocks = [piece[s * ORDER + r : s * ORDER + r + step, :] for s in range(STORED)]
        for k in range(SLOTS):
            total = jnp.where(hits[k][0], blocks[0], 0.0)
            for s in range(1, STORED):
                total = total + jnp.where(hits[k][s], blocks[s], 0.0)
            high = total.astype(jnp.bfloat16)
            low = (total - high.astype(jnp.float32)).astype(jnp.bfloat16)
            write(r, step, k, high, low)


def kernel(
    vals, bcols, rcols, out,
    abuf, bbuf, ad, bhi, blo, cacc, crecv, ostg,
    stage_sem, za_send, za_recv, y_send, y_recv, x_send, x_recv, s_send, s_recv, c_send, c_recv, o_sem,
):
    row, col = lax.axis_index("row"), lax.axis_index("col")
    x, yh, c = lax.div(row, 4), lax.rem(lax.div(row, 2), 2), lax.rem(row, 2)
    z, yl = lax.div(col, 2), lax.rem(col, 2)

    def at_row(x_, yh_, c_):
        return (x_ * 2 + yh_) * 2 + c_

    z_up, z_down = lax.rem(z + 1, NZ), lax.rem(z + NZ - 1, NZ)
    x_up, x_down = lax.rem(x + 1, NX), lax.rem(x + NX - 1, NX)
    sibling = (at_row(x, yh, 1 - c), col)
    partner = (row, z * 2 + 1 - yl)
    z_side = ((row, z_up * 2 + yl), (row, z_down * 2 + yl))
    alone = jnp.logical_and(yh == c, c == yl)

    for p in range(ROWS):
        pltpu.make_async_copy(
            vals.at[p], abuf.at[z, p, pl.ds(0, BODY)], stage_sem.at[p]
        ).start()

    barrier = pltpu.get_barrier_semaphore()

    def greet(device):
        pl.semaphore_signal(barrier, inc=1, device_id=device, device_id_type=MESH)

    greet(z_side[0])
    greet(z_side[1])
    greet((at_row(x_up, yh, c), col))
    greet((at_row(x_down, yh, c), col))
    greet(sibling)
    greet(partner)
    for k in range(2):
        @pl.when(jnp.logical_not(jnp.logical_and(alone, yh == k)))
        def _():
            greet((at_row(x, k, yh), z * 2 + c))
            greet((at_row(x, c, yl), z * 2 + k))

    for p in range(ROWS):
        head = [
            jnp.full((1, ORDER), bcols[s, 0, p].astype(jnp.float32)) for s in range(STORED)
        ]
        head = head + [jnp.zeros((8 - STORED, ORDER), jnp.float32)]
        abuf[z, p, BODY:PIECE, :] = jnp.concatenate(head, axis=0)
    for p in range(ROWS):
        pltpu.make_async_copy(
            vals.at[p], abuf.at[z, p, pl.ds(0, BODY)], stage_sem.at[p]
        ).wait()
    pl.semaphore_wait(barrier, jnp.where(alone, 8, 10))

    def z_copy(way, chain, at, back):
        p, m = lax.div(at, 7) * 2 + chain, lax.rem(at, 7)
        far = lax.div(m, 2) + back
        source = lax.rem(z + (NZ - far if way == 0 else far), NZ)
        for parity in range(2):
            first = parity if way == 0 else 1 - parity
            rows = pl.ds(0, CUT) if first == 0 else pl.ds(CUT, PIECE - CUT)
            ref = abuf.at[source, p, rows]
            yield lax.rem(m, 2) == parity, pltpu.make_async_remote_copy(
                src_ref=ref,
                dst_ref=ref,
                send_sem=za_send.at[way, chain * CHAIN + at],
                recv_sem=za_recv.at[way, chain * CHAIN + at],
                device_id=z_side[way],
                device_id_type=MESH,
            )

    def z_start(way, chain, at):
        for when, copy in z_copy(way, chain, at, 0):
            pl.when(when)(copy.start)

    def z_arrive(way, chain, at):
        for when, copy in z_copy(way, chain, at, 1):
            pl.when(when)(copy.wait_recv)

    def z_sent(way, chain, at):
        for when, copy in z_copy(way, chain, at, 0):
            pl.when(when)(copy.wait_send)

    turn = 1 - 2 * c

    def along_x(steps):
        return lax.rem(x + steps + 4 * NX, NX)

    def x_copy(k, back):
        i = lax.div(k, PHASE) * ROWS + lax.rem(k, ROWS)
        far = lax.div(lax.rem(k, PHASE), ROWS) + back
        ref = bbuf.at[i, along_x(-turn * far) * 2 + c]
        return pltpu.make_async_remote_copy(
            src_ref=ref,
            dst_ref=ref,
            send_sem=x_send.at[k],
            recv_sem=x_recv.at[k],
            device_id=(at_row(along_x(turn), yh, c), col),
            device_id_type=MESH,
        )

    def s_copy(far, i, back):
        slot = along_x(turn * far) * 2 + 1 - c if back else along_x(-turn * far) * 2 + c
        ref = bbuf.at[i, slot]
        return pltpu.make_async_remote_copy(
            src_ref=ref,
            dst_ref=ref,
            send_sem=s_send.at[far, i],
            recv_sem=s_recv.at[far, i],
            device_id=sibling,
            device_id_type=MESH,
        )

    def y_copy(k, p):
        i = jnp.where(c == yl, ROWS, 0) + p
        return pltpu.make_async_remote_copy(
            src_ref=abuf.at[z, p],
            dst_ref=bbuf.at[i, x * 2 + yh],
            send_sem=y_send.at[k, p],
            recv_sem=y_recv.at[i],
            device_id=(at_row(x, k, yh), z * 2 + c),
            device_id_type=MESH,
        )

    def y_local(p):
        return pltpu.make_async_copy(
            abuf.at[z, p], bbuf.at[ROWS + p, x * 2 + yh], y_recv.at[ROWS + p]
        )

    def y_start():
        @pl.loop(0, ROWS)
        def _(p):
            for k in range(2):
                here = jnp.logical_and(alone, yh == k)
                pl.when(here)(lambda: y_local(p).start())
                pl.when(jnp.logical_not(here))(lambda: y_copy(k, p).start())

    def y_arrive(i):
        ref = bbuf.at[i, x * 2 + c]
        own = jnp.logical_and(alone, i >= ROWS)

        @pl.when(own)
        def _():
            y_local(lax.rem(i, ROWS)).wait()

        @pl.when(jnp.logical_not(own))
        def _():
            pltpu.make_async_remote_copy(
                src_ref=ref,
                dst_ref=ref,
                send_sem=y_send.at[0, 0],
                recv_sem=y_recv.at[i],
                device_id=sibling,
                device_id_type=MESH,
            ).wait_recv()

    def c_copy(p):
        return pltpu.make_async_remote_copy(
            src_ref=cacc.at[p],
            dst_ref=crecv.at[p],
            send_sem=c_send.at[p],
            recv_sem=c_recv.at[p],
            device_id=partner,
            device_id_type=MESH,
        )

    def spread_left(source, p):
        mine = lax.rem(source, 2) == c
        far = along_x(jnp.where(mine, turn, -turn) * (x - lax.div(source, 2)) - x)
        lanes = pl.multiple_of(
            (lax.rem(far, 2) * 2 + jnp.where(mine, 0, 1)) * SLOTS * ORDER, SLOTS * ORDER
        )
        unit = p * 2 + lax.div(far, 2)

        def write(r, step, k, high, low):
            at = pl.ds(lanes + k * ORDER, ORDER)
            ad[unit, r : r + step, at] = high
            ad[unit, ORDER + r : ORDER + r + step, at] = low

        spread(abuf.at[source, p], write)

    def spread_right(i, far, other):
        slot = along_x((2 * other - 1) * turn * far) * 2 + jnp.where(other == 1, 1 - c, c)
        base = pl.multiple_of(
            (lax.rem(far, 2) * 2 + other) * SLOTS * ORDER + lax.rem(i, ROWS) * ORDER, ORDER
        )
        unit = lax.div(i, ROWS) * 2 + lax.div(far, 2)

        def write(r, step, k, high, low):
            rows = pl.ds(base + r, step)
            cols = pl.ds(k * ORDER, ORDER)
            bhi[unit, rows, cols] = high
            blo[unit, rows, cols] = low

        spread(bbuf.at[i, slot], write)

    def product(p, phase, half):
        left = ad.at[p * 2 + half]
        both = jnp.dot(left[...], bhi[phase * 2 + half], preferred_element_type=jnp.float32)
        rest = jnp.dot(left[0:ORDER, :], blo[phase * 2 + half], preferred_element_type=jnp.float32)
        total = both[0:ORDER] + (both[ORDER:] + rest)
        at = phase * ROWS + p
        cacc[at] = jnp.where(half == 0, 0.0, cacc[at]) + total

    for at in range(2):
        for way in range(2):
            z_start(way, 0, jnp.int32(at))

    @pl.loop(0, STEPS)
    def _(n):
        even = lax.rem(n, 2) == 0
        chain = jnp.where(n < 4, 0, jnp.where(n < 24, jnp.where(even, 1, 0), 1))
        at = jnp.where(
            n < 4, n, jnp.where(n < 24, lax.div(n + 3, 2) - jnp.where(even, 3, 0), n - CHAIN)
        )
        at = jnp.clip(at, 0, CHAIN - 1)

        @pl.when(n == jnp.where(c == yl, 4, 0))
        def _():
            y_start()

        @pl.when(n < RING)
        def _():
            for way in range(2):
                z_arrive(way, chain, at)

                @pl.when(at + 2 < CHAIN)
                def _():
                    z_start(way, chain, at + 2)

                @pl.when(jnp.logical_or(n == 1, n == 2))
                def _():
                    z_start(way, 1, n - 1)

        k = n - 3

        @pl.when(jnp.logical_and(k >= 0, k < 2 * PHASE))
        def _():
            x_copy(k, 1).wait_recv()

            @pl.when(lax.rem(k, PHASE) < 2 * ROWS)
            def _():
                x_copy(k + ROWS, 0).start()

            i = lax.div(k, PHASE) * ROWS + lax.rem(k, ROWS)
            s_copy(lax.div(lax.rem(k, PHASE), ROWS) + 1, i, 0).start()

        @pl.when(jnp.logical_or(n < ROWS, jnp.logical_and(n >= 11, n < 11 + ROWS)))
        def _():
            i = jnp.where(n < ROWS, n, n - 11 + ROWS)
            y_arrive(i)
            x_copy(lax.div(i, ROWS) * PHASE + lax.rem(i, ROWS), 0).start()
            s_copy(0, i, 0).start()

        def both_cores(far, i):
            s_copy(far, i, 1).wait_recv()

            @pl.loop(0, 2)
            def _(other):
                spread_right(i, far, other)

        own = jnp.logical_or(
            jnp.logical_and(n >= 1, n < 1 + ROWS), jnp.logical_and(n >= 12, n < 12 + ROWS)
        )
        came = jnp.logical_and(n >= 4, n < 4 + 2 * PHASE)
        k_came = jnp.clip(n - 4, 0, 2 * PHASE - 1)
        i_own = jnp.where(n < 1 + ROWS, jnp.maximum(n - 1, 0), n - 12 + ROWS)
        i_came = lax.div(k_came, PHASE) * ROWS + lax.rem(k_came, ROWS)

        @pl.loop(jnp.where(own, 0, 1), jnp.where(came, 2, 1))
        def _(j):
            both_cores(
                jnp.where(j == 0, 0, lax.div(lax.rem(k_came, PHASE), ROWS) + 1),
                jnp.where(j == 0, i_own, i_came),
            )

        @pl.when(n < RING)
        def _():
            p, m = lax.div(at, 7) * 2 + chain, lax.rem(at, 7)
            far = jnp.where(m == 0, 0, lax.div(m + 2, 2))
            count = jnp.where(
                jnp.logical_or(m == 0, m == 6), 1, jnp.where(lax.rem(m, 2) == 1, 2, 0)
            )

            @pl.loop(0, count)
            def _(k):
                source = lax.rem(z + jnp.where(k == 0, far, NZ - far), NZ)
                spread_left(source, p)

        code = jnp.int32(0)
        for at, left_row, phase, half in PRODUCTS:
            code = code + jnp.where(n == at, 1 + left_row * 4 + phase * 2 + half, 0)

        @pl.when(code > 0)
        def _():
            unit = jnp.maximum(code - 1, 0)
            left_row, phase, half = lax.div(unit, 4), lax.rem(lax.div(unit, 2), 2), lax.rem(unit, 2)
            product(left_row, phase, half)

            @pl.when(jnp.logical_and(phase == 0, half == 1))
            def _():
                c_copy(left_row).start()

    @pl.loop(0, ROWS)
    def _(p):
        c_copy(p).wait_recv()
        for u in range(SLOTS):
            want = rcols[p, 0, u]
            for r in range(0, ORDER, 32):
                rows = slice(r, r + 32)
                block = jnp.zeros((32, ORDER), jnp.float32)
                for k in range(SLOTS):
                    cols = slice(k * ORDER, (k + 1) * ORDER)
                    both = cacc[ROWS + p, rows, cols] + crecv[p, rows, cols]
                    block = jnp.where(want == k, both, block)
                ostg[p, u, rows, :] = block
        pltpu.make_async_copy(ostg.at[p], out.at[p, 0], o_sem.at[p]).start()

    @pl.loop(0, CHAIN)
    def _(n):
        for way in range(2):
            for chain in range(2):
                z_sent(way, chain, n)

    @pl.loop(0, ROWS)
    def _(p):
        for k in range(2):
            pl.when(jnp.logical_not(jnp.logical_and(alone, yh == k)))(
                lambda: y_copy(k, p).wait_send()
            )
        c_copy(p).wait_send()

    @pl.loop(0, 2 * ROWS)
    def _(i):
        for far in range(3):
            x_copy(lax.div(i, ROWS) * PHASE + far * ROWS + lax.rem(i, ROWS), 0).wait_send()
        for far in range(4):
            s_copy(far, i, 0).wait_send()

    @pl.loop(0, ROWS)
    def _(p):
        pltpu.make_async_copy(ostg.at[p], out.at[p, 0], o_sem.at[p]).wait()


def on_device(block_values, block_cols, result_cols):
    vals = block_values.reshape(ROWS, BODY, ORDER)
    dma = pltpu.SemaphoreType.DMA
    return pl.pallas_call(
        kernel,
        out_shape=jax.ShapeDtypeStruct((ROWS, 1, SLOTS, ORDER, ORDER), jnp.float32),
        in_specs=[
            pl.BlockSpec(memory_space=pl.ANY),
            pl.BlockSpec(memory_space=pltpu.SMEM),
            pl.BlockSpec(memory_space=pltpu.SMEM),
        ],
        out_specs=pl.BlockSpec(memory_space=pl.ANY),
        scratch_shapes=[
            pltpu.VMEM((NZ, ROWS, PIECE, ORDER), jnp.float32),
            pltpu.VMEM((2 * ROWS, 2 * NX, PIECE, ORDER), jnp.float32),
            pltpu.VMEM((2 * ROWS, 2 * ORDER, NZ * 2 * ORDER), jnp.bfloat16),
            pltpu.VMEM((4, NZ * 2 * ORDER, SLOTS * ORDER), jnp.bfloat16),
            pltpu.VMEM((4, NZ * 2 * ORDER, SLOTS * ORDER), jnp.bfloat16),
            pltpu.VMEM((2 * ROWS, ORDER, SLOTS * ORDER), jnp.float32),
            pltpu.VMEM((ROWS, ORDER, SLOTS * ORDER), jnp.float32),
            pltpu.VMEM((ROWS, SLOTS, ORDER, ORDER), jnp.float32),
            dma((ROWS,)),
            dma((2, RING)),
            dma((2, RING)),
            dma((2, ROWS)),
            dma((2 * ROWS,)),
            dma((2 * PHASE,)),
            dma((2 * PHASE,)),
            dma((4, 2 * ROWS)),
            dma((4, 2 * ROWS)),
            dma((ROWS,)),
            dma((ROWS,)),
            dma((ROWS,)),
        ],
        compiler_params=pltpu.CompilerParams(
            collective_id=0, has_side_effects=True, vmem_limit_bytes=60 * 2**20
        ),
    )(vals, jnp.transpose(block_cols, (2, 1, 0)), result_cols)


def solution(mesh):
    return jax.shard_map(
        on_device,
        mesh=mesh,
        in_specs=(P("row", "col", None, None, None), P("row", "col", None), P("row", "col", None)),
        out_specs=P("row", "col", None, None, None),
        check_vma=False,
    )
```

```python
import functools

import jax
import jax.numpy as jnp
from jax import lax
from jax.experimental import pallas as pl
from jax.experimental.pallas import tpu as pltpu
from jax.sharding import PartitionSpec as P

MESH = pl.DeviceIdType.MESH
NX, NZ = 4, 8
ORDER = 128
STORED, SLOTS, ROWS = 3, 4, 4
BODY = STORED * ORDER
PIECE = BODY + 8
UNITS = 2 * ROWS
HALF = ORDER // 2
PHASE = 3 * ROWS

ALONG_Z = (
    (
        (0, 0), (5, 0), (1, 0), (0, 1), (2, 0), (1, 1), (0, 2),
        (3, 0), (1, 2), (0, 3), (4, 0), (3, 1), (2, 1), (4, 1),
        (3, 2), (2, 2), (4, 2), (3, 3), (7, 0), (4, 3), (6, 0),
        (7, 1), (5, 1), (6, 1), (7, 2), (5, 2), (6, 2), (7, 3),
    ),
    (
        (1, 0), (0, 0), (2, 0), (1, 1), (0, 1), (3, 0), (1, 2),
        (2, 1), (0, 2), (1, 3), (4, 0), (3, 1), (2, 2), (5, 0),
        (4, 1), (2, 3), (6, 0), (3, 2), (4, 2), (5, 1), (6, 1),
        (7, 0), (5, 2), (6, 2), (7, 1), (5, 3), (6, 3), (7, 2),
    ),
)
RING = len(ALONG_Z[0])
HEAD_HOPS = (4, 3)


def schedule():
    starts = []
    for seq in ALONG_Z:
        at = {part: q for q, part in enumerate(seq)}
        issue, own = -1, []
        for q, (u, d) in enumerate(seq):
            if d > 0:
                issue = at[(u, d - 1)]
            else:
                own.append((issue, u))
        starts.append(sorted(own, key=lambda e: e[0]))
    done = [max(q for seq in ALONG_Z for q, (v, _) in enumerate(seq) if v == u) for u in range(UNITS)]
    done = [max(done[2 * p : 2 * p + 2]) for p in range(ROWS)]
    ready = {(0, 0): 7, (0, 1): 15, (1, 0): 19, (1, 1): 27}
    wanted = [(phase, p, half) for phase in range(2) for p in range(ROWS) for half in range(2)]
    wanted = [w for w in wanted if w[0] == 1 or w[1] < ROWS - 1]
    rows, n = [], 7
    while wanted:
        can = [w for w in wanted if max(done[w[1]], ready[(w[0], w[2])]) <= n]
        if can and n != RING - 1:
            rows.append((n,) + can[0])
            wanted.remove(can[0])
        n += 1
    units = []
    for u in range(UNITS - 2, UNITS):
        units.append((max(u, 16), u, 0))
        for way, seq in enumerate(ALONG_Z):
            units += [
                (max(q, 16), u, (NZ - d - 1 if way == 0 else d + 1) % NZ)
                for q, (v, d) in enumerate(seq)
                if v == u
            ]
    return starts, rows, sorted(units, key=lambda e: e[0]), n


STARTS, ROW_PRODUCTS, UNIT_PRODUCTS, STEPS = schedule()


def lookup(n, values):
    found = jnp.int32(0)
    for at, value in values:
        found = found + jnp.where(n == at, value, 0)
    return found


def before(n, steps):
    count = jnp.int32(0)
    for at in steps:
        count = count + jnp.where(n > at, 1, 0)
    return count


def spread(block, head, rows, write):
    step = 32
    hits = [
        [jnp.broadcast_to(head(s), (step, ORDER)) == float(k) for s in range(STORED)]
        for k in range(SLOTS)
    ]
    for r in range(0, rows, step):
        blocks = [block(s, pl.ds(r, step)) for s in range(STORED)]
        for k in range(SLOTS):
            total = jnp.where(hits[k][0], blocks[0], 0.0)
            for s in range(1, STORED):
                total = total + jnp.where(hits[k][s], blocks[s], 0.0)
            high = total.astype(jnp.bfloat16)
            low = (total - high.astype(jnp.float32)).astype(jnp.bfloat16)
            write(r, step, k, high, low)


def kernel(
    vals, bcols, rcols, out,
    abuf, hdr, stage, bbuf, ad, bhi, blo, cacc, crecv,
    stage_sem, unit_sem, h_send, h_recv, za_send, za_recv, y_send, y_recv, x_send, x_recv, s_send, s_recv, c_send, c_recv,
):
    row, col = lax.axis_index("row"), lax.axis_index("col")
    x, yh, c = lax.div(row, 4), lax.rem(lax.div(row, 2), 2), lax.rem(row, 2)
    z, yl = lax.div(col, 2), lax.rem(col, 2)

    def at_row(x_, yh_, c_):
        return (x_ * 2 + yh_) * 2 + c_

    z_up, z_down = lax.rem(z + 1, NZ), lax.rem(z + NZ - 1, NZ)
    x_up, x_down = lax.rem(x + 1, NX), lax.rem(x + NX - 1, NX)
    sibling = (at_row(x, yh, 1 - c), col)
    partner = (row, z * 2 + 1 - yl)
    z_side = ((row, z_up * 2 + yl), (row, z_down * 2 + yl))
    alone = jnp.logical_and(yh == c, c == yl)

    def unit_load(u, s):
        p, part = lax.div(u, 2), lax.rem(u, 2)
        rows = pl.ds(pl.multiple_of(s * ORDER + part * HALF, HALF), HALF)
        return pltpu.make_async_copy(
            vals.at[p, rows], abuf.at[z, u, s], unit_sem.at[u, s]
        )

    def row_load(p):
        return pltpu.make_async_copy(
            vals.at[p], stage.at[p, pl.ds(0, BODY)], stage_sem.at[p]
        )

    @pl.loop(0, UNITS)
    def _(u):
        for s in range(STORED):
            unit_load(u, s).start()

    @pl.loop(0, ROWS)
    def _(p):
        row_load(p).start()

    barrier = pltpu.get_barrier_semaphore()

    def greet(device):
        pl.semaphore_signal(barrier, inc=1, device_id=device, device_id_type=MESH)

    greet(z_side[0])
    greet(z_side[1])
    greet((at_row(x_up, yh, c), col))
    greet((at_row(x_down, yh, c), col))
    greet(sibling)
    greet(partner)
    for k in range(2):
        @pl.when(jnp.logical_not(jnp.logical_and(alone, yh == k)))
        def _():
            greet((at_row(x, k, yh), z * 2 + c))
            greet((at_row(x, c, yl), z * 2 + k))

    for p in range(ROWS):
        for s in range(8):
            name = bcols[s, 0, p].astype(jnp.float32) if s < STORED else jnp.float32(0)
            line = jnp.full((1, ORDER), name)
            if s < 4:
                hdr[z, p * 4 + s : p * 4 + s + 1, :] = line
            stage[p, BODY + s : BODY + s + 1, :] = line

    @pl.loop(0, 2 * ROWS)
    def _(at):
        cacc[at] = jnp.zeros((ORDER, SLOTS * ORDER), jnp.float32)

    @pl.loop(0, UNITS)
    def _(u):
        for s in range(STORED):
            unit_load(u, s).wait()

    @pl.loop(0, ROWS)
    def _(p):
        row_load(p).wait()

    pl.semaphore_wait(barrier, jnp.where(alone, 8, 10))

    def behind(way, far):
        return lax.rem(z + (NZ - far if way == 0 else far), NZ)

    def z_copy(way, u, d, back):
        ref = abuf.at[behind(way, d + back), u]
        return pltpu.make_async_remote_copy(
            src_ref=ref,
            dst_ref=ref,
            send_sem=za_send.at[way, u * 4 + d],
            recv_sem=za_recv.at[way, u * 4 + d],
            device_id=z_side[way],
            device_id_type=MESH,
        )

    def h_copy(way, d, back):
        ref = hdr.at[behind(way, d + back)]
        return pltpu.make_async_remote_copy(
            src_ref=ref,
            dst_ref=ref,
            send_sem=h_send.at[way, d],
            recv_sem=h_recv.at[way, d],
            device_id=z_side[way],
            device_id_type=MESH,
        )

    turn = 1 - 2 * c

    def along_x(steps):
        return lax.rem(x + steps + 4 * NX, NX)

    def x_copy(k, back):
        i = lax.div(k, PHASE) * ROWS + lax.rem(k, ROWS)
        far = lax.div(lax.rem(k, PHASE), ROWS) + back
        ref = bbuf.at[i, along_x(-turn * far) * 2 + c]
        return pltpu.make_async_remote_copy(
            src_ref=ref,
            dst_ref=ref,
            send_sem=x_send.at[k],
            recv_sem=x_recv.at[k],
            device_id=(at_row(along_x(turn), yh, c), col),
            device_id_type=MESH,
        )

    def s_copy(far, i, back):
        slot = along_x(turn * far) * 2 + 1 - c if back else along_x(-turn * far) * 2 + c
        ref = bbuf.at[i, slot]
        return pltpu.make_async_remote_copy(
            src_ref=ref,
            dst_ref=ref,
            send_sem=s_send.at[far, i],
            recv_sem=s_recv.at[far, i],
            device_id=sibling,
            device_id_type=MESH,
        )

    def y_copy(k, p):
        i = jnp.where(c == yl, ROWS, 0) + p
        return pltpu.make_async_remote_copy(
            src_ref=stage.at[p],
            dst_ref=bbuf.at[i, x * 2 + yh],
            send_sem=y_send.at[k, p],
            recv_sem=y_recv.at[i],
            device_id=(at_row(x, k, yh), z * 2 + c),
            device_id_type=MESH,
        )

    def y_local(p):
        return pltpu.make_async_copy(
            stage.at[p], bbuf.at[ROWS + p, x * 2 + yh], y_recv.at[ROWS + p]
        )

    def y_start():
        @pl.loop(0, ROWS)
        def _(p):
            for k in range(2):
                here = jnp.logical_and(alone, yh == k)
                pl.when(here)(lambda: y_local(p).start())
                pl.when(jnp.logical_not(here))(lambda: y_copy(k, p).start())

    def y_arrive(i):
        ref = bbuf.at[i, x * 2 + c]
        own = jnp.logical_and(alone, i >= ROWS)

        @pl.when(own)
        def _():
            y_local(lax.rem(i, ROWS)).wait()

        @pl.when(jnp.logical_not(own))
        def _():
            pltpu.make_async_remote_copy(
                src_ref=ref,
                dst_ref=ref,
                send_sem=y_send.at[0, 0],
                recv_sem=y_recv.at[i],
                device_id=sibling,
                device_id_type=MESH,
            ).wait_recv()

    def half_row(u):
        return pl.ds(pl.multiple_of(lax.rem(u, 2) * HALF, HALF), HALF)

    def c_copy(u):
        return pltpu.make_async_remote_copy(
            src_ref=cacc.at[lax.div(u, 2), half_row(u)],
            dst_ref=crecv.at[lax.div(u, 2), half_row(u)],
            send_sem=c_send.at[u],
            recv_sem=c_recv.at[u],
            device_id=partner,
            device_id_type=MESH,
        )

    def spread_left(u, source):
        p, part = lax.div(u, 2), lax.rem(u, 2)
        high_at = pl.multiple_of(HALF + part * HALF, HALF)
        low_at = pl.multiple_of(part * 3 * HALF, HALF)

        def write(r, step, k, high, low):
            cols = pl.ds(k * ORDER, ORDER)
            ad[p, source, pl.ds(high_at + r, step), cols] = high
            ad[p, source, pl.ds(low_at + r, step), cols] = low

        spread(
            lambda s, rows: abuf[source, u, s, rows, :],
            lambda s: hdr[source, pl.ds(p * 4 + s, 1), :],
            HALF,
            write,
        )

    def right_slot(far, other):
        return along_x((2 * other - 1) * turn * far) * 2 + jnp.where(other == 1, 1 - c, c)

    def spread_right(i, far, other):
        slot = right_slot(far, other)
        base = pl.multiple_of(lax.rem(i, ROWS) * ORDER, ORDER)
        phase = lax.div(i, ROWS)

        def write(r, step, k, high, low):
            rows = pl.ds(base + r, step)
            cols = pl.ds(k * ORDER, ORDER)
            bhi[phase, slot, rows, cols] = high
            blo[phase, slot, rows, cols] = low

        spread(
            lambda s, rows: bbuf[i, slot, pl.ds(s * ORDER + rows.start, rows.size), :],
            lambda s: bbuf[i, slot, BODY + s : BODY + s + 1, :],
            ORDER,
            write,
        )

    def dot(left, right):
        return jnp.dot(left, right, preferred_element_type=jnp.float32)

    def row_product(phase, p, half):
        @pl.loop(0, 4)
        def _(j):
            slot = right_slot(half * 2 + lax.div(j, 2), lax.rem(j, 2))
            both = dot(ad[p, slot], bhi[phase, slot])
            rest = dot(ad[p, slot, HALF : 3 * HALF, :], blo[phase, slot])
            at = phase * ROWS + p
            cacc[at, 0:HALF, :] += both[0:HALF] + both[HALF : 2 * HALF] + rest[0:HALF]
            cacc[at, HALF:ORDER, :] += (
                both[2 * HALF : 3 * HALF] + both[3 * HALF :] + rest[HALF:]
            )

    def unit_product(u, source):
        p, part = lax.div(u, 2), lax.rem(u, 2)
        whole = pl.ds(pl.multiple_of(part * ORDER, ORDER), ORDER)
        highs = pl.ds(pl.multiple_of(HALF + part * HALF, HALF), HALF)
        both = dot(ad[p, source, whole, :], bhi[0, source])
        rest = dot(ad[p, source, highs, :], blo[0, source])
        cacc[p, half_row(u), :] += both[0:HALF] + both[HALF:] + rest

    for way in range(2):
        h_copy(way, 0, 0).start()
    for way in range(2):
        for at, u in STARTS[way]:
            if at < 0:
                z_copy(way, u, 0, 0).start()

    @pl.loop(0, STEPS)
    def _(n):
        arrived = [
            lookup(n, [(q, u * 4 + d) for q, (u, d) in enumerate(seq)]) for seq in ALONG_Z
        ]

        @pl.when(n == jnp.where(c == yl, 4, 0))
        def _():
            y_start()

        for d in range(4):
            @pl.when(n == 3 * d)
            def _():
                for way in range(2):
                    if d < HEAD_HOPS[way]:
                        h_copy(way, d, 1).wait_recv()
                    if d + 1 < HEAD_HOPS[way]:
                        h_copy(way, d + 1, 0).start()

        @pl.when(n < RING)
        def _():
            for way in range(2):
                u, d = lax.div(arrived[way], 4), lax.rem(arrived[way], 4)
                z_copy(way, u, d, 1).wait_recv()
                last = lookup(
                    u, [(v, sum(part[0] == v for part in ALONG_Z[way]) - 1) for v in range(UNITS)]
                )

                @pl.when(d < last)
                def _():
                    z_copy(way, u, d + 1, 0).start()

                steps = [at for at, _ in STARTS[way]]

                @pl.loop(before(n, steps), before(n + 1, steps))
                def _(j):
                    own = lookup(j, [(e, v) for e, (_, v) in enumerate(STARTS[way])])
                    z_copy(way, own, 0, 0).start()

        k = n - 3

        @pl.when(jnp.logical_and(k >= 0, k < 2 * PHASE))
        def _():
            x_copy(k, 1).wait_recv()

            @pl.when(lax.rem(k, PHASE) < 2 * ROWS)
            def _():
                x_copy(k + ROWS, 0).start()

            i = lax.div(k, PHASE) * ROWS + lax.rem(k, ROWS)
            s_copy(lax.div(lax.rem(k, PHASE), ROWS) + 1, i, 0).start()

        @pl.when(jnp.logical_or(n < ROWS, jnp.logical_and(n >= 11, n < 11 + ROWS)))
        def _():
            i = jnp.where(n < ROWS, n, n - 11 + ROWS)
            y_arrive(i)
            x_copy(lax.div(i, ROWS) * PHASE + lax.rem(i, ROWS), 0).start()
            s_copy(0, i, 0).start()

        def both_cores(far, i):
            s_copy(far, i, 1).wait_recv()

            @pl.loop(0, 2)
            def _(other):
                spread_right(i, far, other)

        own = jnp.logical_or(
            jnp.logical_and(n >= 1, n < 1 + ROWS), jnp.logical_and(n >= 12, n < 12 + ROWS)
        )
        came = jnp.logical_and(n >= 4, n < 4 + 2 * PHASE)
        k_came = jnp.clip(n - 4, 0, 2 * PHASE - 1)
        i_own = jnp.where(n < 1 + ROWS, jnp.maximum(n - 1, 0), n - 12 + ROWS)
        i_came = lax.div(k_came, PHASE) * ROWS + lax.rem(k_came, ROWS)

        @pl.loop(jnp.where(own, 0, 1), jnp.where(came, 2, 1))
        def _(j):
            both_cores(
                jnp.where(j == 0, 0, lax.div(lax.rem(k_came, PHASE), ROWS) + 1),
                jnp.where(j == 0, i_own, i_came),
            )

        @pl.loop(jnp.where(n < RING, 0, 3), jnp.where(n < UNITS, 3, jnp.where(n < RING, 2, 3)))
        def _(j):
            part = jnp.where(j == 0, arrived[0], jnp.where(j == 1, arrived[1], n * 4))
            far = lax.rem(part, 4) + 1
            away = jnp.where(j == 0, NZ - far, jnp.where(j == 1, far, 0))
            spread_left(lax.div(part, 4), lax.rem(z + away, NZ))

        steps = [at for at, _, _ in UNIT_PRODUCTS]

        @pl.loop(before(n, steps), before(n + 1, steps))
        def _(j):
            code = lookup(j, [(e, u * NZ + a) for e, (_, u, a) in enumerate(UNIT_PRODUCTS)])
            unit_product(lax.div(code, NZ), lax.rem(z + lax.rem(code, NZ), NZ))

        for u in range(UNITS - 2, UNITS):
            @pl.when(n == max(at for at, v, _ in UNIT_PRODUCTS if v == u))
            def _():
                c_copy(u).start()

        code = lookup(n, [(at, 1 + phase * 8 + p * 2 + half) for at, phase, p, half in ROW_PRODUCTS])

        @pl.when(code > 0)
        def _():
            unit = jnp.maximum(code - 1, 0)
            phase, p, half = lax.div(unit, 8), lax.rem(lax.div(unit, 2), ROWS), lax.rem(unit, 2)
            row_product(phase, p, half)

            @pl.when(jnp.logical_and(phase == 0, half == 1))
            def _():
                c_copy(p * 2).start()
                c_copy(p * 2 + 1).start()

    for way in range(2):
        for d in range(HEAD_HOPS[way]):
            h_copy(way, d, 0).wait_send()

        @pl.loop(0, RING)
        def _(n):
            part = lookup(n, [(q, u * 4 + d) for q, (u, d) in enumerate(ALONG_Z[way])])
            z_copy(way, lax.div(part, 4), lax.rem(part, 4), 0).wait_send()

    @pl.loop(0, ROWS)
    def _(p):
        for k in range(2):
            pl.when(jnp.logical_not(jnp.logical_and(alone, yh == k)))(
                lambda: y_copy(k, p).wait_send()
            )

    @pl.loop(0, 2 * ROWS)
    def _(i):
        for far in range(3):
            x_copy(lax.div(i, ROWS) * PHASE + far * ROWS + lax.rem(i, ROWS), 0).wait_send()
        for far in range(4):
            s_copy(far, i, 0).wait_send()

    @pl.loop(0, ROWS)
    def _(p):
        c_copy(p * 2).wait_recv()
        c_copy(p * 2 + 1).wait_recv()
        for u in range(SLOTS):
            want = rcols[p, 0, u]
            for r in range(0, ORDER, 32):
                rows = slice(r, r + 32)
                block = jnp.zeros((32, ORDER), jnp.float32)
                for k in range(SLOTS):
                    cols = slice(k * ORDER, (k + 1) * ORDER)
                    both = cacc[ROWS + p, rows, cols] + crecv[p, rows, cols]
                    block = jnp.where(want == k, both, block)
                out[p, 0, u, rows, :] = block

    @pl.loop(0, UNITS)
    def _(u):
        c_copy(u).wait_send()


def on_device(block_values, block_cols, result_cols):
    vals = block_values.reshape(ROWS, BODY, ORDER)
    dma = pltpu.SemaphoreType.DMA
    return pl.pallas_call(
        kernel,
        out_shape=pltpu.VMEM((ROWS, 1, SLOTS, ORDER, ORDER), jnp.float32),
        in_specs=[
            pl.BlockSpec(memory_space=pl.ANY),
            pl.BlockSpec(memory_space=pltpu.SMEM),
            pl.BlockSpec(memory_space=pltpu.SMEM),
        ],
        out_specs=pl.BlockSpec(memory_space=pltpu.VMEM),
        scratch_shapes=[
            pltpu.VMEM((NZ, UNITS, STORED, HALF, ORDER), jnp.float32),
            pltpu.VMEM((NZ, 4 * ROWS, ORDER), jnp.float32),
            pltpu.VMEM((ROWS, PIECE, ORDER), jnp.float32),
            pltpu.VMEM((2 * ROWS, 2 * NX, PIECE, ORDER), jnp.float32),
            pltpu.VMEM((ROWS, NZ, 2 * ORDER, SLOTS * ORDER), jnp.bfloat16),
            pltpu.VMEM((2, NZ, SLOTS * ORDER, SLOTS * ORDER), jnp.bfloat16),
            pltpu.VMEM((2, NZ, SLOTS * ORDER, SLOTS * ORDER), jnp.bfloat16),
            pltpu.VMEM((2 * ROWS, ORDER, SLOTS * ORDER), jnp.float32),
            pltpu.VMEM((ROWS, ORDER, SLOTS * ORDER), jnp.float32),
            dma((ROWS,)),
            dma((UNITS, STORED)),
            dma((2, 4)),
            dma((2, 4)),
            dma((2, 4 * UNITS)),
            dma((2, 4 * UNITS)),
            dma((2, ROWS)),
            dma((2 * ROWS,)),
            dma((2 * PHASE,)),
            dma((2 * PHASE,)),
            dma((4, 2 * ROWS)),
            dma((4, 2 * ROWS)),
            dma((UNITS,)),
            dma((UNITS,)),
        ],
        compiler_params=pltpu.CompilerParams(
            collective_id=0, has_side_effects=True, vmem_limit_bytes=60 * 2**20
        ),
    )(vals, jnp.transpose(block_cols, (2, 1, 0)), result_cols)


def solution(mesh):
    return jax.shard_map(
        on_device,
        mesh=mesh,
        in_specs=(P("row", "col", None, None, None), P("row", "col", None), P("row", "col", None)),
        out_specs=P("row", "col", None, None, None),
        check_vma=False,
    )
```

```python
import functools

import jax
import jax.numpy as jnp
from jax import lax
from jax.experimental import pallas as pl
from jax.experimental.pallas import tpu as pltpu
from jax.sharding import PartitionSpec as P

MESH = pl.DeviceIdType.MESH
NX, NZ = 4, 8
ORDER = 128
STORED, SLOTS, ROWS = 3, 4, 4
BODY = STORED * ORDER
PIECE = BODY + 8
UNITS = 2 * ROWS
HALF = ORDER // 2
PHASE = 3 * ROWS
EARLY = 22

ALONG_Z = (
    (
        (0, 0), (1, 0), (0, 1), (1, 1), (2, 0), (0, 2), (3, 0),
        (1, 2), (0, 3), (2, 1), (3, 1), (4, 0), (2, 2), (5, 0),
        (3, 2), (2, 3), (4, 1), (5, 1), (6, 0), (4, 2), (5, 2),
        (6, 1), (4, 3), (7, 0), (6, 2), (7, 1), (6, 3), (7, 2),
    ),
    (
        (1, 0), (0, 0), (1, 1), (0, 1), (3, 0), (1, 2), (2, 0),
        (0, 2), (1, 3), (3, 1), (2, 1), (5, 0), (3, 2), (4, 0),
        (2, 2), (3, 3), (5, 1), (4, 1), (7, 0), (5, 2), (6, 0),
        (4, 2), (5, 3), (7, 1), (6, 1), (7, 2), (6, 2), (7, 3),
    ),
)
RING = len(ALONG_Z[0])
HEAD_HOPS = (4, 3)


def schedule():
    starts = []
    for seq in ALONG_Z:
        at = {part: q for q, part in enumerate(seq)}
        issue, own = -1, []
        for q, (u, d) in enumerate(seq):
            if d > 0:
                issue = at[(u, d - 1)]
            else:
                own.append((issue, u))
        starts.append(sorted(own, key=lambda e: e[0]))
    done = [max(q for seq in ALONG_Z for q, (v, _) in enumerate(seq) if v == u) for u in range(UNITS)]
    done = [max(done[2 * p : 2 * p + 2]) for p in range(ROWS)]
    ready = {(0, 0): 6, (0, 2): 14, (1, 0): 18, (1, 2): 22, (1, 3): 26}
    wanted = [(0, p, q, 2) for p in range(ROWS - 1) for q in (0, 2)]
    wanted += [(1, p, 0, 2) for p in range(ROWS - 1)]
    wanted += [(1, p, q, 1) for q in (2, 3) for p in range(ROWS - 1)]
    wanted += [(1, ROWS - 1, q, 2) for q in (0, 2)]
    rows = []
    for n in range(RING + 1):
        room = 2 if n < RING else 4 * ROWS * ROWS
        for w in list(wanted):
            open_at = max(done[w[1]], *(ready.get((w[0], q), 0) for q in range(w[2], w[2] + w[3])))
            if open_at <= n and w[3] <= room:
                rows.append((n,) + w)
                wanted.remove(w)
                room -= w[3]
    units = []
    for u in range(UNITS - 2, UNITS):
        units.append((max(u, 16), u, 0))
        for way, seq in enumerate(ALONG_Z):
            units += [
                (max(q, 16), u, (NZ - d - 1 if way == 0 else d + 1) % NZ)
                for q, (v, d) in enumerate(seq)
                if v == u
            ]
    return starts, rows, sorted(units, key=lambda e: e[0])


STARTS, ROW_PRODUCTS, UNIT_PRODUCTS = schedule()
STEPS = RING + 1


def lookup(n, values):
    found = jnp.int32(0)
    for at, value in values:
        found = found + jnp.where(n == at, value, 0)
    return found


def before(n, steps):
    count = jnp.int32(0)
    for at in steps:
        count = count + jnp.where(n > at, 1, 0)
    return count


def spread(block, head, rows, write):
    step = 32
    hits = [
        [jnp.broadcast_to(head(s), (step, ORDER)) == float(k) for s in range(STORED)]
        for k in range(SLOTS)
    ]
    for r in range(0, rows, step):
        blocks = [block(s, pl.ds(r, step)) for s in range(STORED)]
        for k in range(SLOTS):
            total = jnp.where(hits[k][0], blocks[0], 0.0)
            for s in range(1, STORED):
                total = total + jnp.where(hits[k][s], blocks[s], 0.0)
            high = total.astype(jnp.bfloat16)
            low = (total - high.astype(jnp.float32)).astype(jnp.bfloat16)
            write(r, step, k, high, low)


def kernel(
    vals, bcols, rcols, out,
    abuf, hdr, stage, bbuf, ad, bhi, blo, cacc, crecv,
    stage_sem, unit_sem, h_send, h_recv, za_send, za_recv, y_send, y_recv, x_send, x_recv, s_send, s_recv, c_send, c_recv,
):
    row, col = lax.axis_index("row"), lax.axis_index("col")
    x, yh, c = lax.div(row, 4), lax.rem(lax.div(row, 2), 2), lax.rem(row, 2)
    z, yl = lax.div(col, 2), lax.rem(col, 2)

    def at_row(x_, yh_, c_):
        return (x_ * 2 + yh_) * 2 + c_

    z_up, z_down = lax.rem(z + 1, NZ), lax.rem(z + NZ - 1, NZ)
    x_up, x_down = lax.rem(x + 1, NX), lax.rem(x + NX - 1, NX)
    sibling = (at_row(x, yh, 1 - c), col)
    partner = (row, z * 2 + 1 - yl)
    z_side = ((row, z_up * 2 + yl), (row, z_down * 2 + yl))
    alone = jnp.logical_and(yh == c, c == yl)

    def unit_load(u, s):
        p, part = lax.div(u, 2), lax.rem(u, 2)
        rows = pl.ds(pl.multiple_of(s * ORDER + part * HALF, HALF), HALF)
        return pltpu.make_async_copy(
            vals.at[p, rows], abuf.at[z, u, s], unit_sem.at[u, s]
        )

    def row_load(p):
        return pltpu.make_async_copy(
            vals.at[p], stage.at[p, pl.ds(0, BODY)], stage_sem.at[p]
        )

    @pl.loop(0, UNITS)
    def _(u):
        for s in range(STORED):
            unit_load(u, s).start()

    @pl.loop(0, ROWS)
    def _(p):
        row_load(p).start()

    barrier = pltpu.get_barrier_semaphore()

    def greet(device):
        pl.semaphore_signal(barrier, inc=1, device_id=device, device_id_type=MESH)

    greet(z_side[0])
    greet(z_side[1])
    greet((at_row(x_up, yh, c), col))
    greet((at_row(x_down, yh, c), col))
    greet(sibling)
    greet(partner)
    for k in range(2):
        @pl.when(jnp.logical_not(jnp.logical_and(alone, yh == k)))
        def _():
            greet((at_row(x, k, yh), z * 2 + c))
            greet((at_row(x, c, yl), z * 2 + k))

    for p in range(ROWS):
        for s in range(8):
            name = bcols[s, 0, p].astype(jnp.float32) if s < STORED else jnp.float32(0)
            line = jnp.full((1, ORDER), name)
            if s < 4:
                hdr[z, p * 4 + s : p * 4 + s + 1, :] = line
            stage[p, BODY + s : BODY + s + 1, :] = line

    @pl.loop(0, 2 * ROWS)
    def _(at):
        cacc[at] = jnp.zeros((ORDER, SLOTS * ORDER), jnp.float32)

    @pl.loop(0, UNITS)
    def _(u):
        for s in range(STORED):
            unit_load(u, s).wait()

    @pl.loop(0, ROWS)
    def _(p):
        row_load(p).wait()

    pl.semaphore_wait(barrier, jnp.where(alone, 8, 10))

    def behind(way, far):
        return lax.rem(z + (NZ - far if way == 0 else far), NZ)

    def z_copy(way, u, d, back):
        ref = abuf.at[behind(way, d + back), u]
        return pltpu.make_async_remote_copy(
            src_ref=ref,
            dst_ref=ref,
            send_sem=za_send.at[way, u * 4 + d],
            recv_sem=za_recv.at[way, u * 4 + d],
            device_id=z_side[way],
            device_id_type=MESH,
        )

    def h_copy(way, d, back):
        ref = hdr.at[behind(way, d + back)]
        return pltpu.make_async_remote_copy(
            src_ref=ref,
            dst_ref=ref,
            send_sem=h_send.at[way, d],
            recv_sem=h_recv.at[way, d],
            device_id=z_side[way],
            device_id_type=MESH,
        )

    turn = 1 - 2 * c

    def along_x(steps):
        return lax.rem(x + steps + 4 * NX, NX)

    def x_copy(k, back):
        i = lax.div(k, PHASE) * ROWS + lax.rem(k, ROWS)
        far = lax.div(lax.rem(k, PHASE), ROWS) + back
        ref = bbuf.at[i, along_x(-turn * far) * 2 + c]
        return pltpu.make_async_remote_copy(
            src_ref=ref,
            dst_ref=ref,
            send_sem=x_send.at[k],
            recv_sem=x_recv.at[k],
            device_id=(at_row(along_x(turn), yh, c), col),
            device_id_type=MESH,
        )

    def s_copy(far, i, back):
        slot = along_x(turn * far) * 2 + 1 - c if back else along_x(-turn * far) * 2 + c
        ref = bbuf.at[i, slot]
        return pltpu.make_async_remote_copy(
            src_ref=ref,
            dst_ref=ref,
            send_sem=s_send.at[far, i],
            recv_sem=s_recv.at[far, i],
            device_id=sibling,
            device_id_type=MESH,
        )

    def y_copy(k, p):
        i = jnp.where(c == yl, ROWS, 0) + p
        return pltpu.make_async_remote_copy(
            src_ref=stage.at[p],
            dst_ref=bbuf.at[i, x * 2 + yh],
            send_sem=y_send.at[k, p],
            recv_sem=y_recv.at[i],
            device_id=(at_row(x, k, yh), z * 2 + c),
            device_id_type=MESH,
        )

    def y_local(p):
        return pltpu.make_async_copy(
            stage.at[p], bbuf.at[ROWS + p, x * 2 + yh], y_recv.at[ROWS + p]
        )

    def y_start():
        @pl.loop(0, ROWS)
        def _(p):
            for k in range(2):
                here = jnp.logical_and(alone, yh == k)
                pl.when(here)(lambda: y_local(p).start())
                pl.when(jnp.logical_not(here))(lambda: y_copy(k, p).start())

    def y_arrive(i):
        ref = bbuf.at[i, x * 2 + c]
        own = jnp.logical_and(alone, i >= ROWS)

        @pl.when(own)
        def _():
            y_local(lax.rem(i, ROWS)).wait()

        @pl.when(jnp.logical_not(own))
        def _():
            pltpu.make_async_remote_copy(
                src_ref=ref,
                dst_ref=ref,
                send_sem=y_send.at[0, 0],
                recv_sem=y_recv.at[i],
                device_id=sibling,
                device_id_type=MESH,
            ).wait_recv()

    def half_row(u):
        return pl.ds(pl.multiple_of(lax.rem(u, 2) * HALF, HALF), HALF)

    def c_copy(u):
        return pltpu.make_async_remote_copy(
            src_ref=cacc.at[lax.div(u, 2), half_row(u)],
            dst_ref=crecv.at[lax.div(u, 2), half_row(u)],
            send_sem=c_send.at[u],
            recv_sem=c_recv.at[u],
            device_id=partner,
            device_id_type=MESH,
        )

    def left_slot(source):
        mine = lax.rem(source, 2) == c
        far = along_x(jnp.where(mine, turn, -turn) * (x - lax.div(source, 2)) - x)
        return far * 2 + jnp.where(mine, 0, 1)

    def in_half(slot):
        return pl.multiple_of(lax.rem(slot, 4) * SLOTS * ORDER, SLOTS * ORDER)

    def spread_left(u, source):
        p, part = lax.div(u, 2), lax.rem(u, 2)
        high_at = pl.multiple_of(HALF + part * HALF, HALF)
        low_at = pl.multiple_of(part * 3 * HALF, HALF)
        slot = left_slot(source)
        lanes = in_half(slot)
        unit = p * 2 + lax.div(slot, 4)

        def write(r, step, k, high, low):
            cols = pl.ds(lanes + k * ORDER, ORDER)
            ad[unit, pl.ds(high_at + r, step), cols] = high
            ad[unit, pl.ds(low_at + r, step), cols] = low

        spread(
            lambda s, rows: abuf[source, u, s, rows, :],
            lambda s: hdr[source, pl.ds(p * 4 + s, 1), :],
            HALF,
            write,
        )

    def right_slot(far, other):
        return along_x((2 * other - 1) * turn * far) * 2 + jnp.where(other == 1, 1 - c, c)

    def spread_right(i, far, other):
        slot = right_slot(far, other)
        base = pl.multiple_of(in_half(far * 2 + other) + lax.rem(i, ROWS) * ORDER, ORDER)
        unit = lax.div(i, ROWS) * 2 + lax.div(far, 2)

        def write(r, step, k, high, low):
            rows = pl.ds(base + r, step)
            cols = pl.ds(k * ORDER, ORDER)
            bhi[unit, rows, cols] = high
            blo[unit, rows, cols] = low

        spread(
            lambda s, rows: bbuf[i, slot, pl.ds(s * ORDER + rows.start, rows.size), :],
            lambda s: bbuf[i, slot, BODY + s : BODY + s + 1, :],
            ORDER,
            write,
        )

    def dot(left, right):
        return jnp.dot(left, right, preferred_element_type=jnp.float32)

    def row_product(phase, p, half, inner):
        both = dot(ad[p * 2 + half, :, inner], bhi[phase * 2 + half, inner, :])
        rest = dot(ad[p * 2 + half, HALF : 3 * HALF, inner], blo[phase * 2 + half, inner, :])
        at = phase * ROWS + p
        cacc[at, 0:HALF, :] += both[0:HALF] + both[HALF : 2 * HALF] + rest[0:HALF]
        cacc[at, HALF:ORDER, :] += (
            both[2 * HALF : 3 * HALF] + both[3 * HALF :] + rest[HALF:]
        )

    def unit_product(u, source):
        p, part = lax.div(u, 2), lax.rem(u, 2)
        whole = pl.ds(pl.multiple_of(part * ORDER, ORDER), ORDER)
        highs = pl.ds(pl.multiple_of(HALF + part * HALF, HALF), HALF)
        slot = left_slot(source)
        inner = pl.ds(in_half(slot), SLOTS * ORDER)
        half = lax.div(slot, 4)
        both = dot(ad[p * 2 + half, whole, inner], bhi[half, inner, :])
        rest = dot(ad[p * 2 + half, highs, inner], blo[half, inner, :])
        cacc[p, half_row(u), :] += both[0:HALF] + both[HALF:] + rest

    def z_sent(u):
        for way, seq in enumerate(ALONG_Z):
            for d in range(sum(part[0] == u for part in seq)):
                z_copy(way, u, d, 0).wait_send()

    def y_sent(p):
        for k in range(2):
            pl.when(jnp.logical_not(jnp.logical_and(alone, yh == k)))(
                lambda: y_copy(k, p).wait_send()
            )

    def x_sent(k):
        x_copy(k, 0).wait_send()
        i = lax.div(k, PHASE) * ROWS + lax.rem(k, ROWS)
        s_copy(lax.div(lax.rem(k, PHASE), ROWS) + 1, i, 0).wait_send()

    for way in range(2):
        h_copy(way, 0, 0).start()
    for way in range(2):
        for at, u in STARTS[way]:
            if at < 0:
                z_copy(way, u, 0, 0).start()

    @pl.loop(0, STEPS)
    def _(n):
        arrived = [
            lookup(n, [(q, u * 4 + d) for q, (u, d) in enumerate(seq)]) for seq in ALONG_Z
        ]

        @pl.when(n == jnp.where(c == yl, 4, 0))
        def _():
            y_start()

        for d in range(4):
            @pl.when(n == (0, 2, 5, 8)[d])
            def _():
                for way in range(2):
                    if d < HEAD_HOPS[way]:
                        h_copy(way, d, 1).wait_recv()
                    if d + 1 < HEAD_HOPS[way]:
                        h_copy(way, d + 1, 0).start()

        @pl.when(n < RING)
        def _():
            for way in range(2):
                u, d = lax.div(arrived[way], 4), lax.rem(arrived[way], 4)
                z_copy(way, u, d, 1).wait_recv()
                last = lookup(
                    u, [(v, sum(part[0] == v for part in ALONG_Z[way]) - 1) for v in range(UNITS)]
                )

                @pl.when(d < last)
                def _():
                    z_copy(way, u, d + 1, 0).start()

                steps = [at for at, _ in STARTS[way]]

                @pl.loop(before(n, steps), before(n + 1, steps))
                def _(j):
                    own = lookup(j, [(e, v) for e, (_, v) in enumerate(STARTS[way])])
                    z_copy(way, own, 0, 0).start()

        k = n - 2

        @pl.when(jnp.logical_and(k >= 0, k < 2 * PHASE))
        def _():
            x_copy(k, 1).wait_recv()

            @pl.when(lax.rem(k, PHASE) < 2 * ROWS)
            def _():
                x_copy(k + ROWS, 0).start()

            i = lax.div(k, PHASE) * ROWS + lax.rem(k, ROWS)
            s_copy(lax.div(lax.rem(k, PHASE), ROWS) + 1, i, 0).start()

        @pl.when(jnp.logical_or(n < ROWS, jnp.logical_and(n >= 10, n < 10 + ROWS)))
        def _():
            i = jnp.where(n < ROWS, n, n - 10 + ROWS)
            y_arrive(i)
            x_copy(lax.div(i, ROWS) * PHASE + lax.rem(i, ROWS), 0).start()
            s_copy(0, i, 0).start()

        def both_cores(far, i):
            s_copy(far, i, 1).wait_recv()

            @pl.loop(0, 2)
            def _(other):
                spread_right(i, far, other)

        own = jnp.logical_or(
            jnp.logical_and(n >= 1, n < 1 + ROWS), jnp.logical_and(n >= 11, n < 11 + ROWS)
        )
        came = jnp.logical_and(n >= 3, n < 3 + 2 * PHASE)
        k_came = jnp.clip(n - 3, 0, 2 * PHASE - 1)
        i_own = jnp.where(n < 1 + ROWS, jnp.maximum(n - 1, 0), n - 11 + ROWS)
        i_came = lax.div(k_came, PHASE) * ROWS + lax.rem(k_came, ROWS)

        @pl.loop(jnp.where(own, 0, 1), jnp.where(came, 2, 1))
        def _(j):
            both_cores(
                jnp.where(j == 0, 0, lax.div(lax.rem(k_came, PHASE), ROWS) + 1),
                jnp.where(j == 0, i_own, i_came),
            )

        @pl.loop(jnp.where(n < RING, 0, 3), jnp.where(n < UNITS, 3, jnp.where(n < RING, 2, 3)))
        def _(j):
            part = jnp.where(j == 0, arrived[0], jnp.where(j == 1, arrived[1], n * 4))
            far = lax.rem(part, 4) + 1
            away = jnp.where(j == 0, NZ - far, jnp.where(j == 1, far, 0))
            spread_left(lax.div(part, 4), lax.rem(z + away, NZ))

        steps = [at for at, _, _ in UNIT_PRODUCTS]

        @pl.loop(before(n, steps), before(n + 1, steps))
        def _(j):
            code = lookup(j, [(e, u * NZ + a) for e, (_, u, a) in enumerate(UNIT_PRODUCTS)])
            unit_product(lax.div(code, NZ), lax.rem(z + lax.rem(code, NZ), NZ))

        for u in range(UNITS - 2, UNITS):
            @pl.when(n == max(at for at, v, _ in UNIT_PRODUCTS if v == u))
            def _():
                c_copy(u).start()

        for u in range(UNITS - 2):
            @pl.when(n == 20 + u)
            def _():
                z_sent(u)

        @pl.when(jnp.logical_and(n >= 6, n < 6 + EARLY))
        def _():
            x_sent(n - 6)

        @pl.when(jnp.logical_and(n >= 18, n < 18 + 2 * ROWS))
        def _():
            s_copy(0, n - 18, 0).wait_send()

        @pl.when(jnp.logical_and(n >= 16, n < 16 + ROWS))
        def _():
            y_sent(n - 16)

        @pl.when(n == 15)
        def _():
            for way in range(2):
                for d in range(HEAD_HOPS[way]):
                    h_copy(way, d, 0).wait_send()

        row_steps = [e[0] for e in ROW_PRODUCTS]

        @pl.loop(before(n, row_steps), before(n + 1, row_steps))
        def _(j):
            code = lookup(
                j,
                [
                    (e, ((phase * ROWS + p) * 4 + q) * 2 + count - 1)
                    for e, (_, phase, p, q, count) in enumerate(ROW_PRODUCTS)
                ],
            )
            row, quarter = lax.div(code, 8), lax.rem(lax.div(code, 2), 4)
            phase, p, half = lax.div(row, ROWS), lax.rem(row, ROWS), lax.div(quarter, 2)
            depth = 2 * SLOTS * ORDER

            @pl.when(lax.rem(code, 2) == 1)
            def _():
                row_product(phase, p, half, pl.ds(0, 2 * depth))

            @pl.when(lax.rem(code, 2) == 0)
            def _():
                start = pl.multiple_of(lax.rem(quarter, 2) * depth, depth)
                row_product(phase, p, half, pl.ds(start, depth))

            @pl.when(jnp.logical_and(phase == 0, half == 1))
            def _():
                c_copy(p * 2).start()
                c_copy(p * 2 + 1).start()

    for u in range(UNITS - 2, UNITS):
        z_sent(u)

    @pl.loop(EARLY, 2 * PHASE)
    def _(k):
        x_sent(k)

    @pl.loop(0, ROWS)
    def _(p):
        c_copy(p * 2).wait_recv()
        c_copy(p * 2 + 1).wait_recv()
        wants = [rcols[p, 0, u] for u in range(SLOTS)]
        for r in range(0, ORDER, 32):
            rows = slice(r, r + 32)
            both = [
                cacc[ROWS + p, rows, k * ORDER : (k + 1) * ORDER]
                + crecv[p, rows, k * ORDER : (k + 1) * ORDER]
                for k in range(SLOTS)
            ]
            for u in range(SLOTS):
                block = both[0]
                for k in range(1, SLOTS):
                    block = jnp.where(wants[u] == k, both[k], block)
                out[p, 0, u, rows, :] = block

    @pl.loop(0, UNITS)
    def _(u):
        c_copy(u).wait_send()


def on_device(block_values, block_cols, result_cols):
    vals = block_values.reshape(ROWS, BODY, ORDER)
    dma = pltpu.SemaphoreType.DMA
    return pl.pallas_call(
        kernel,
        out_shape=pltpu.VMEM((ROWS, 1, SLOTS, ORDER, ORDER), jnp.float32),
        in_specs=[
            pl.BlockSpec(memory_space=pl.ANY),
            pl.BlockSpec(memory_space=pltpu.SMEM),
            pl.BlockSpec(memory_space=pltpu.SMEM),
        ],
        out_specs=pl.BlockSpec(memory_space=pltpu.VMEM),
        scratch_shapes=[
            pltpu.VMEM((NZ, UNITS, STORED, HALF, ORDER), jnp.float32),
            pltpu.VMEM((NZ, 4 * ROWS, ORDER), jnp.float32),
            pltpu.VMEM((ROWS, PIECE, ORDER), jnp.float32),
            pltpu.VMEM((2 * ROWS, 2 * NX, PIECE, ORDER), jnp.float32),
            pltpu.VMEM((2 * ROWS, 2 * ORDER, 4 * SLOTS * ORDER), jnp.bfloat16),
            pltpu.VMEM((4, 4 * SLOTS * ORDER, SLOTS * ORDER), jnp.bfloat16),
            pltpu.VMEM((4, 4 * SLOTS * ORDER, SLOTS * ORDER), jnp.bfloat16),
            pltpu.VMEM((2 * ROWS, ORDER, SLOTS * ORDER), jnp.float32),
            pltpu.VMEM((ROWS, ORDER, SLOTS * ORDER), jnp.float32),
            dma((ROWS,)),
            dma((UNITS, STORED)),
            dma((2, 4)),
            dma((2, 4)),
            dma((2, 4 * UNITS)),
            dma((2, 4 * UNITS)),
            dma((2, ROWS)),
            dma((2 * ROWS,)),
            dma((2 * PHASE,)),
            dma((2 * PHASE,)),
            dma((4, 2 * ROWS)),
            dma((4, 2 * ROWS)),
            dma((UNITS,)),
            dma((UNITS,)),
        ],
        compiler_params=pltpu.CompilerParams(
            collective_id=0, has_side_effects=True, vmem_limit_bytes=60 * 2**20
        ),
    )(vals, jnp.transpose(block_cols, (2, 1, 0)), result_cols)


def solution(mesh):
    return jax.shard_map(
        on_device,
        mesh=mesh,
        in_specs=(P("row", "col", None, None, None), P("row", "col", None), P("row", "col", None)),
        out_specs=P("row", "col", None, None, None),
        check_vma=False,
    )
```

```python
import functools

import jax
import jax.numpy as jnp
from jax import lax
from jax.experimental import pallas as pl
from jax.experimental.pallas import tpu as pltpu
from jax.sharding import PartitionSpec as P

MESH = pl.DeviceIdType.MESH
NX, NZ = 4, 8
ORDER = 128
STORED, SLOTS, ROWS = 3, 4, 4
BODY = STORED * ORDER
PIECE = BODY + 8
UNITS = 2 * ROWS
HALF = ORDER // 2
PHASE = 3 * ROWS
EARLY = 22

ALONG_Z = (
    (
        (0, 0), (1, 0), (0, 1), (1, 1), (2, 0), (0, 2), (3, 0),
        (1, 2), (0, 3), (2, 1), (3, 1), (4, 0), (2, 2), (5, 0),
        (3, 2), (2, 3), (4, 1), (5, 1), (6, 0), (4, 2), (5, 2),
        (6, 1), (4, 3), (7, 0), (6, 2), (7, 1), (6, 3), (7, 2),
    ),
    (
        (1, 0), (0, 0), (1, 1), (0, 1), (3, 0), (1, 2), (2, 0),
        (0, 2), (1, 3), (3, 1), (2, 1), (5, 0), (3, 2), (4, 0),
        (2, 2), (3, 3), (5, 1), (4, 1), (7, 0), (5, 2), (6, 0),
        (4, 2), (5, 3), (7, 1), (6, 1), (7, 2), (6, 2), (7, 3),
    ),
)
RING = len(ALONG_Z[0])
HEAD_HOPS = (4, 3)


def schedule():
    starts = []
    for seq in ALONG_Z:
        at = {part: q for q, part in enumerate(seq)}
        issue, own = -1, []
        for q, (u, d) in enumerate(seq):
            if d > 0:
                issue = at[(u, d - 1)]
            else:
                own.append((issue, u))
        starts.append(sorted(own, key=lambda e: e[0]))
    done = [max(q for seq in ALONG_Z for q, (v, _) in enumerate(seq) if v == u) for u in range(UNITS)]
    done = [max(done[2 * p : 2 * p + 2]) for p in range(ROWS)]
    ready = {(0, 0): 6, (0, 2): 14, (1, 0): 18, (1, 2): 22, (1, 3): 26}
    wanted = [(0, p, q, 2) for p in range(ROWS - 1) for q in (0, 2)]
    wanted += [(1, p, 0, 2) for p in range(ROWS - 1)]
    wanted += [(1, p, q, 1) for q in (2, 3) for p in range(ROWS - 1)]
    wanted += [(1, ROWS - 1, q, 2) for q in (0, 2)]
    rows = []
    for n in range(RING + 1):
        room = 2 if n < RING else 4 * ROWS * ROWS
        for w in list(wanted):
            open_at = max(done[w[1]], *(ready.get((w[0], q), 0) for q in range(w[2], w[2] + w[3])))
            if open_at <= n and w[3] <= room:
                rows.append((n,) + w)
                wanted.remove(w)
                room -= w[3]
    units = []
    for u in range(UNITS - 2, UNITS):
        units.append((max(u, 16), u, 0))
        for way, seq in enumerate(ALONG_Z):
            units += [
                (max(q, 16), u, (NZ - d - 1 if way == 0 else d + 1) % NZ)
                for q, (v, d) in enumerate(seq)
                if v == u
            ]
    return starts, rows, sorted(units, key=lambda e: e[0])


STARTS, ROW_PRODUCTS, UNIT_PRODUCTS = schedule()
STEPS = RING + 1


def lookup(n, values):
    found = jnp.int32(0)
    for at, value in values:
        found = found + jnp.where(n == at, value, 0)
    return found


def before(n, steps):
    count = jnp.int32(0)
    for at in steps:
        count = count + jnp.where(n > at, 1, 0)
    return count


def spread(block, head, rows, write):
    step = 64
    hits = [
        [jnp.broadcast_to(head(s), (step, ORDER)) == float(k) for s in range(STORED)]
        for k in range(SLOTS)
    ]
    for r in range(0, rows, step):
        blocks = [block(s, pl.ds(r, step)) for s in range(STORED)]
        for k in range(SLOTS):
            total = jnp.where(hits[k][0], blocks[0], 0.0)
            for s in range(1, STORED):
                total = total + jnp.where(hits[k][s], blocks[s], 0.0)
            high = total.astype(jnp.bfloat16)
            low = (total - high.astype(jnp.float32)).astype(jnp.bfloat16)
            write(r, step, k, high, low)


def kernel(
    vals, bcols, rcols, out,
    abuf, hdr, stage, bbuf, ad, bhi, blo, cacc, crecv,
    stage_sem, unit_sem, h_send, h_recv, za_send, za_recv, y_send, y_recv, x_send, x_recv, s_send, s_recv, c_send, c_recv,
):
    row, col = lax.axis_index("row"), lax.axis_index("col")
    x, yh, c = lax.div(row, 4), lax.rem(lax.div(row, 2), 2), lax.rem(row, 2)
    z, yl = lax.div(col, 2), lax.rem(col, 2)

    def at_row(x_, yh_, c_):
        return (x_ * 2 + yh_) * 2 + c_

    z_up, z_down = lax.rem(z + 1, NZ), lax.rem(z + NZ - 1, NZ)
    x_up, x_down = lax.rem(x + 1, NX), lax.rem(x + NX - 1, NX)
    sibling = (at_row(x, yh, 1 - c), col)
    partner = (row, z * 2 + 1 - yl)
    z_side = ((row, z_up * 2 + yl), (row, z_down * 2 + yl))
    alone = jnp.logical_and(yh == c, c == yl)

    def unit_load(u, s):
        p, part = lax.div(u, 2), lax.rem(u, 2)
        rows = pl.ds(pl.multiple_of(s * ORDER + part * HALF, HALF), HALF)
        return pltpu.make_async_copy(
            vals.at[p, rows], abuf.at[z, u, s], unit_sem.at[u, s]
        )

    def row_load(p):
        return pltpu.make_async_copy(
            vals.at[p], stage.at[p, pl.ds(0, BODY)], stage_sem.at[p]
        )

    @pl.loop(0, UNITS)
    def _(u):
        for s in range(STORED):
            unit_load(u, s).start()

    @pl.loop(0, ROWS)
    def _(p):
        row_load(p).start()

    barrier = pltpu.get_barrier_semaphore()

    def greet(device):
        pl.semaphore_signal(barrier, inc=1, device_id=device, device_id_type=MESH)

    greet(z_side[0])
    greet(z_side[1])
    greet((at_row(x_up, yh, c), col))
    greet((at_row(x_down, yh, c), col))
    greet(sibling)
    greet(partner)
    for k in range(2):
        @pl.when(jnp.logical_not(jnp.logical_and(alone, yh == k)))
        def _():
            greet((at_row(x, k, yh), z * 2 + c))
            greet((at_row(x, c, yl), z * 2 + k))

    for p in range(ROWS):
        for s in range(8):
            name = bcols[s, 0, p].astype(jnp.float32) if s < STORED else jnp.float32(0)
            line = jnp.full((1, ORDER), name)
            if s < 4:
                hdr[z, p * 4 + s : p * 4 + s + 1, :] = line
            stage[p, BODY + s : BODY + s + 1, :] = line

    @pl.loop(0, 2 * ROWS)
    def _(at):
        cacc[at] = jnp.zeros((ORDER, SLOTS * ORDER), jnp.float32)

    @pl.loop(0, UNITS)
    def _(u):
        for s in range(STORED):
            unit_load(u, s).wait()

    @pl.loop(0, ROWS)
    def _(p):
        row_load(p).wait()

    pl.semaphore_wait(barrier, jnp.where(alone, 8, 10))

    def behind(way, far):
        return lax.rem(z + (NZ - far if way == 0 else far), NZ)

    def z_copy(way, u, d, back):
        ref = abuf.at[behind(way, d + back), u]
        return pltpu.make_async_remote_copy(
            src_ref=ref,
            dst_ref=ref,
            send_sem=za_send.at[way, u * 4 + d],
            recv_sem=za_recv.at[way, u * 4 + d],
            device_id=z_side[way],
            device_id_type=MESH,
        )

    def h_copy(way, d, back):
        ref = hdr.at[behind(way, d + back)]
        return pltpu.make_async_remote_copy(
            src_ref=ref,
            dst_ref=ref,
            send_sem=h_send.at[way, d],
            recv_sem=h_recv.at[way, d],
            device_id=z_side[way],
            device_id_type=MESH,
        )

    turn = 1 - 2 * c

    def along_x(steps):
        return lax.rem(x + steps + 4 * NX, NX)

    def x_copy(k, back):
        i = lax.div(k, PHASE) * ROWS + lax.rem(k, ROWS)
        far = lax.div(lax.rem(k, PHASE), ROWS) + back
        ref = bbuf.at[i, along_x(-turn * far) * 2 + c]
        return pltpu.make_async_remote_copy(
            src_ref=ref,
            dst_ref=ref,
            send_sem=x_send.at[k],
            recv_sem=x_recv.at[k],
            device_id=(at_row(along_x(turn), yh, c), col),
            device_id_type=MESH,
        )

    def s_copy(far, i, back):
        slot = along_x(turn * far) * 2 + 1 - c if back else along_x(-turn * far) * 2 + c
        ref = bbuf.at[i, slot]
        return pltpu.make_async_remote_copy(
            src_ref=ref,
            dst_ref=ref,
            send_sem=s_send.at[far, i],
            recv_sem=s_recv.at[far, i],
            device_id=sibling,
            device_id_type=MESH,
        )

    def y_copy(k, p):
        i = jnp.where(c == yl, ROWS, 0) + p
        return pltpu.make_async_remote_copy(
            src_ref=stage.at[p],
            dst_ref=bbuf.at[i, x * 2 + yh],
            send_sem=y_send.at[k, p],
            recv_sem=y_recv.at[i],
            device_id=(at_row(x, k, yh), z * 2 + c),
            device_id_type=MESH,
        )

    def y_local(p):
        return pltpu.make_async_copy(
            stage.at[p], bbuf.at[ROWS + p, x * 2 + yh], y_recv.at[ROWS + p]
        )

    def y_start():
        @pl.loop(0, ROWS)
        def _(p):
            for k in range(2):
                here = jnp.logical_and(alone, yh == k)
                pl.when(here)(lambda: y_local(p).start())
                pl.when(jnp.logical_not(here))(lambda: y_copy(k, p).start())

    def y_arrive(i):
        ref = bbuf.at[i, x * 2 + c]
        own = jnp.logical_and(alone, i >= ROWS)

        @pl.when(own)
        def _():
            y_local(lax.rem(i, ROWS)).wait()

        @pl.when(jnp.logical_not(own))
        def _():
            pltpu.make_async_remote_copy(
                src_ref=ref,
                dst_ref=ref,
                send_sem=y_send.at[0, 0],
                recv_sem=y_recv.at[i],
                device_id=sibling,
                device_id_type=MESH,
            ).wait_recv()

    def half_row(u):
        return pl.ds(pl.multiple_of(lax.rem(u, 2) * HALF, HALF), HALF)

    def c_copy(u):
        return pltpu.make_async_remote_copy(
            src_ref=cacc.at[lax.div(u, 2), half_row(u)],
            dst_ref=crecv.at[lax.div(u, 2), half_row(u)],
            send_sem=c_send.at[u],
            recv_sem=c_recv.at[u],
            device_id=partner,
            device_id_type=MESH,
        )

    def left_slot(source):
        mine = lax.rem(source, 2) == c
        far = along_x(jnp.where(mine, turn, -turn) * (x - lax.div(source, 2)) - x)
        return far * 2 + jnp.where(mine, 0, 1)

    def in_half(slot):
        return pl.multiple_of(lax.rem(slot, 4) * SLOTS * ORDER, SLOTS * ORDER)

    def spread_left(u, source):
        p, part = lax.div(u, 2), lax.rem(u, 2)
        high_at = pl.multiple_of(HALF + part * HALF, HALF)
        low_at = pl.multiple_of(part * 3 * HALF, HALF)
        slot = left_slot(source)
        lanes = in_half(slot)
        unit = p * 2 + lax.div(slot, 4)

        def write(r, step, k, high, low):
            cols = pl.ds(lanes + k * ORDER, ORDER)
            ad[unit, pl.ds(high_at + r, step), cols] = high
            ad[unit, pl.ds(low_at + r, step), cols] = low

        spread(
            lambda s, rows: abuf[source, u, s, rows, :],
            lambda s: hdr[source, pl.ds(p * 4 + s, 1), :],
            HALF,
            write,
        )

    def right_slot(far, other):
        return along_x((2 * other - 1) * turn * far) * 2 + jnp.where(other == 1, 1 - c, c)

    def spread_right(i, far, other):
        slot = right_slot(far, other)
        base = pl.multiple_of(in_half(far * 2 + other) + lax.rem(i, ROWS) * ORDER, ORDER)
        unit = lax.div(i, ROWS) * 2 + lax.div(far, 2)

        def write(r, step, k, high, low):
            rows = pl.ds(base + r, step)
            cols = pl.ds(k * ORDER, ORDER)
            bhi[unit, rows, cols] = high
            blo[unit, rows, cols] = low

        spread(
            lambda s, rows: bbuf[i, slot, pl.ds(s * ORDER + rows.start, rows.size), :],
            lambda s: bbuf[i, slot, BODY + s : BODY + s + 1, :],
            ORDER,
            write,
        )

    def dot(left, right):
        return jnp.dot(left, right, preferred_element_type=jnp.float32)

    def row_product(phase, p, half, inner):
        both = dot(ad[p * 2 + half, :, inner], bhi[phase * 2 + half, inner, :])
        rest = dot(ad[p * 2 + half, HALF : 3 * HALF, inner], blo[phase * 2 + half, inner, :])
        at = phase * ROWS + p
        cacc[at, 0:HALF, :] += both[0:HALF] + both[HALF : 2 * HALF] + rest[0:HALF]
        cacc[at, HALF:ORDER, :] += (
            both[2 * HALF : 3 * HALF] + both[3 * HALF :] + rest[HALF:]
        )

    def unit_product(u, source):
        p, part = lax.div(u, 2), lax.rem(u, 2)
        whole = pl.ds(pl.multiple_of(part * ORDER, ORDER), ORDER)
        highs = pl.ds(pl.multiple_of(HALF + part * HALF, HALF), HALF)
        slot = left_slot(source)
        inner = pl.ds(in_half(slot), SLOTS * ORDER)
        half = lax.div(slot, 4)
        both = dot(ad[p * 2 + half, whole, inner], bhi[half, inner, :])
        rest = dot(ad[p * 2 + half, highs, inner], blo[half, inner, :])
        cacc[p, half_row(u), :] += both[0:HALF] + both[HALF:] + rest

    def z_sent(u):
        for way, seq in enumerate(ALONG_Z):
            for d in range(sum(part[0] == u for part in seq)):
                z_copy(way, u, d, 0).wait_send()

    def y_sent(p):
        for k in range(2):
            pl.when(jnp.logical_not(jnp.logical_and(alone, yh == k)))(
                lambda: y_copy(k, p).wait_send()
            )

    def x_sent(k):
        x_copy(k, 0).wait_send()
        i = lax.div(k, PHASE) * ROWS + lax.rem(k, ROWS)
        s_copy(lax.div(lax.rem(k, PHASE), ROWS) + 1, i, 0).wait_send()

    for way in range(2):
        h_copy(way, 0, 0).start()
    for way in range(2):
        for at, u in STARTS[way]:
            if at < 0:
                z_copy(way, u, 0, 0).start()

    @pl.loop(0, STEPS)
    def _(n):
        arrived = [
            lookup(n, [(q, u * 4 + d) for q, (u, d) in enumerate(seq)]) for seq in ALONG_Z
        ]

        @pl.when(n == jnp.where(c == yl, 4, 0))
        def _():
            y_start()

        @pl.when(jnp.logical_or(n < ROWS, jnp.logical_and(n >= 10, n < 10 + ROWS)))
        def _():
            i = jnp.where(n < ROWS, n, n - 10 + ROWS)
            y_arrive(i)
            x_copy(lax.div(i, ROWS) * PHASE + lax.rem(i, ROWS), 0).start()
            s_copy(0, i, 0).start()

        for d in range(4):
            @pl.when(n == (0, 2, 5, 8)[d])
            def _():
                for way in range(2):
                    if d < HEAD_HOPS[way]:
                        h_copy(way, d, 1).wait_recv()
                    if d + 1 < HEAD_HOPS[way]:
                        h_copy(way, d + 1, 0).start()

        @pl.when(n < RING)
        def _():
            for way in range(2):
                u, d = lax.div(arrived[way], 4), lax.rem(arrived[way], 4)
                z_copy(way, u, d, 1).wait_recv()
                last = lookup(
                    u, [(v, sum(part[0] == v for part in ALONG_Z[way]) - 1) for v in range(UNITS)]
                )

                @pl.when(d < last)
                def _():
                    z_copy(way, u, d + 1, 0).start()

                steps = [at for at, _ in STARTS[way]]

                @pl.loop(before(n, steps), before(n + 1, steps))
                def _(j):
                    own = lookup(j, [(e, v) for e, (_, v) in enumerate(STARTS[way])])
                    z_copy(way, own, 0, 0).start()

        k = n - 2

        @pl.when(jnp.logical_and(k >= 0, k < 2 * PHASE))
        def _():
            x_copy(k, 1).wait_recv()

            @pl.when(lax.rem(k, PHASE) < 2 * ROWS)
            def _():
                x_copy(k + ROWS, 0).start()

            i = lax.div(k, PHASE) * ROWS + lax.rem(k, ROWS)
            s_copy(lax.div(lax.rem(k, PHASE), ROWS) + 1, i, 0).start()

        @pl.loop(jnp.where(n < RING, 0, 3), jnp.where(n < UNITS, 3, jnp.where(n < RING, 2, 3)))
        def _(j):
            part = jnp.where(j == 0, arrived[0], jnp.where(j == 1, arrived[1], n * 4))
            far = lax.rem(part, 4) + 1
            away = jnp.where(j == 0, NZ - far, jnp.where(j == 1, far, 0))
            spread_left(lax.div(part, 4), lax.rem(z + away, NZ))

        steps = [at for at, _, _ in UNIT_PRODUCTS]

        @pl.loop(before(n, steps), before(n + 1, steps))
        def _(j):
            code = lookup(j, [(e, u * NZ + a) for e, (_, u, a) in enumerate(UNIT_PRODUCTS)])
            unit_product(lax.div(code, NZ), lax.rem(z + lax.rem(code, NZ), NZ))

        for u in range(UNITS - 2, UNITS):
            @pl.when(n == max(at for at, v, _ in UNIT_PRODUCTS if v == u))
            def _():
                c_copy(u).start()

        def both_cores(far, i):
            s_copy(far, i, 1).wait_recv()

            @pl.loop(0, 2)
            def _(other):
                spread_right(i, far, other)

        own = jnp.logical_or(
            jnp.logical_and(n >= 1, n < 1 + ROWS), jnp.logical_and(n >= 11, n < 11 + ROWS)
        )
        came = jnp.logical_and(n >= 3, n < 3 + 2 * PHASE)
        k_came = jnp.clip(n - 3, 0, 2 * PHASE - 1)
        i_own = jnp.where(n < 1 + ROWS, jnp.maximum(n - 1, 0), n - 11 + ROWS)
        i_came = lax.div(k_came, PHASE) * ROWS + lax.rem(k_came, ROWS)

        @pl.loop(jnp.where(own, 0, 1), jnp.where(came, 2, 1))
        def _(j):
            both_cores(
                jnp.where(j == 0, 0, lax.div(lax.rem(k_came, PHASE), ROWS) + 1),
                jnp.where(j == 0, i_own, i_came),
            )

        for u in range(UNITS - 2):
            @pl.when(n == 20 + u)
            def _():
                z_sent(u)

        @pl.when(jnp.logical_and(n >= 6, n < 6 + EARLY))
        def _():
            x_sent(n - 6)

        @pl.when(jnp.logical_and(n >= 18, n < 18 + 2 * ROWS))
        def _():
            s_copy(0, n - 18, 0).wait_send()

        @pl.when(jnp.logical_and(n >= 16, n < 16 + ROWS))
        def _():
            y_sent(n - 16)

        @pl.when(n == 15)
        def _():
            for way in range(2):
                for d in range(HEAD_HOPS[way]):
                    h_copy(way, d, 0).wait_send()

        row_steps = [e[0] for e in ROW_PRODUCTS]

        @pl.loop(before(n, row_steps), before(n + 1, row_steps))
        def _(j):
            code = lookup(
                j,
                [
                    (e, ((phase * ROWS + p) * 4 + q) * 2 + count - 1)
                    for e, (_, phase, p, q, count) in enumerate(ROW_PRODUCTS)
                ],
            )
            row, quarter = lax.div(code, 8), lax.rem(lax.div(code, 2), 4)
            phase, p, half = lax.div(row, ROWS), lax.rem(row, ROWS), lax.div(quarter, 2)
            depth = 2 * SLOTS * ORDER

            @pl.when(lax.rem(code, 2) == 1)
            def _():
                row_product(phase, p, half, pl.ds(0, 2 * depth))

            @pl.when(lax.rem(code, 2) == 0)
            def _():
                start = pl.multiple_of(lax.rem(quarter, 2) * depth, depth)
                row_product(phase, p, half, pl.ds(start, depth))

            @pl.when(jnp.logical_and(phase == 0, half == 1))
            def _():
                c_copy(p * 2).start()
                c_copy(p * 2 + 1).start()

    for u in range(UNITS - 2, UNITS):
        z_sent(u)

    @pl.loop(EARLY, 2 * PHASE)
    def _(k):
        x_sent(k)

    @pl.loop(0, ROWS)
    def _(p):
        c_copy(p * 2).wait_recv()
        c_copy(p * 2 + 1).wait_recv()
        wants = [rcols[p, 0, u] for u in range(SLOTS)]
        for r in range(0, ORDER, 32):
            rows = slice(r, r + 32)
            both = [
                cacc[ROWS + p, rows, k * ORDER : (k + 1) * ORDER]
                + crecv[p, rows, k * ORDER : (k + 1) * ORDER]
                for k in range(SLOTS)
            ]
            for u in range(SLOTS):
                block = both[0]
                for k in range(1, SLOTS):
                    block = jnp.where(wants[u] == k, both[k], block)
                out[p, 0, u, rows, :] = block

    @pl.loop(0, UNITS)
    def _(u):
        c_copy(u).wait_send()


def on_device(block_values, block_cols, result_cols):
    vals = block_values.reshape(ROWS, BODY, ORDER)
    dma = pltpu.SemaphoreType.DMA
    return pl.pallas_call(
        kernel,
        out_shape=pltpu.VMEM((ROWS, 1, SLOTS, ORDER, ORDER), jnp.float32),
        in_specs=[
            pl.BlockSpec(memory_space=pl.ANY),
            pl.BlockSpec(memory_space=pltpu.SMEM),
            pl.BlockSpec(memory_space=pltpu.SMEM),
        ],
        out_specs=pl.BlockSpec(memory_space=pltpu.VMEM),
        scratch_shapes=[
            pltpu.VMEM((NZ, UNITS, STORED, HALF, ORDER), jnp.float32),
            pltpu.VMEM((NZ, 4 * ROWS, ORDER), jnp.float32),
            pltpu.VMEM((ROWS, PIECE, ORDER), jnp.float32),
            pltpu.VMEM((2 * ROWS, 2 * NX, PIECE, ORDER), jnp.float32),
            pltpu.VMEM((2 * ROWS, 2 * ORDER, 4 * SLOTS * ORDER), jnp.bfloat16),
            pltpu.VMEM((4, 4 * SLOTS * ORDER, SLOTS * ORDER), jnp.bfloat16),
            pltpu.VMEM((4, 4 * SLOTS * ORDER, SLOTS * ORDER), jnp.bfloat16),
            pltpu.VMEM((2 * ROWS, ORDER, SLOTS * ORDER), jnp.float32),
            pltpu.VMEM((ROWS, ORDER, SLOTS * ORDER), jnp.float32),
            dma((ROWS,)),
            dma((UNITS, STORED)),
            dma((2, 4)),
            dma((2, 4)),
            dma((2, 4 * UNITS)),
            dma((2, 4 * UNITS)),
            dma((2, ROWS)),
            dma((2 * ROWS,)),
            dma((2 * PHASE,)),
            dma((2 * PHASE,)),
            dma((4, 2 * ROWS)),
            dma((4, 2 * ROWS)),
            dma((UNITS,)),
            dma((UNITS,)),
        ],
        compiler_params=pltpu.CompilerParams(
            collective_id=0, has_side_effects=True, vmem_limit_bytes=60 * 2**20
        ),
    )(vals, jnp.transpose(block_cols, (2, 1, 0)), result_cols)


def solution(mesh):
    return jax.shard_map(
        on_device,
        mesh=mesh,
        in_specs=(P("row", "col", None, None, None), P("row", "col", None), P("row", "col", None)),
        out_specs=P("row", "col", None, None, None),
        check_vma=False,
    )
```

```python
import functools

import jax
import jax.numpy as jnp
from jax import lax
from jax.experimental import pallas as pl
from jax.experimental.pallas import tpu as pltpu
from jax.sharding import PartitionSpec as P

MESH = pl.DeviceIdType.MESH
NX, NZ = 4, 8
ORDER = 128
STORED, SLOTS, ROWS = 3, 4, 4
BODY = STORED * ORDER
PIECE = BODY + 8
UNITS = 2 * ROWS
HALF = ORDER // 2
PHASE = 3 * ROWS
EARLY = 22

ALONG_Z = (
    (
        (0, 0), (1, 0), (0, 1), (1, 1), (2, 0), (0, 2), (3, 0),
        (1, 2), (0, 3), (2, 1), (3, 1), (4, 0), (2, 2), (5, 0),
        (3, 2), (2, 3), (4, 1), (5, 1), (6, 0), (4, 2), (5, 2),
        (6, 1), (4, 3), (7, 0), (6, 2), (7, 1), (6, 3), (7, 2),
    ),
    (
        (1, 0), (0, 0), (1, 1), (0, 1), (3, 0), (1, 2), (2, 0),
        (0, 2), (1, 3), (3, 1), (2, 1), (5, 0), (3, 2), (4, 0),
        (2, 2), (3, 3), (5, 1), (4, 1), (7, 0), (5, 2), (6, 0),
        (4, 2), (5, 3), (7, 1), (6, 1), (7, 2), (6, 2), (7, 3),
    ),
)
RING = len(ALONG_Z[0])
HEAD_HOPS = (4, 3)


def schedule():
    starts = []
    for seq in ALONG_Z:
        at = {part: q for q, part in enumerate(seq)}
        issue, own = -1, []
        for q, (u, d) in enumerate(seq):
            if d > 0:
                issue = at[(u, d - 1)]
            else:
                own.append((issue, u))
        starts.append(sorted(own, key=lambda e: e[0]))
    done = [max(q for seq in ALONG_Z for q, (v, _) in enumerate(seq) if v == u) for u in range(UNITS)]
    done = [max(done[2 * p : 2 * p + 2]) for p in range(ROWS)]
    ready = {(0, 0): 6, (0, 2): 14, (1, 0): 18, (1, 2): 22, (1, 3): 26}
    wanted = [(0, p, q, 2) for p in range(ROWS - 1) for q in (0, 2)]
    wanted += [(1, p, 0, 2) for p in range(ROWS - 1)]
    wanted += [(1, p, q, 1) for q in (2, 3) for p in range(ROWS - 1)]
    wanted += [(1, ROWS - 1, q, 2) for q in (0, 2)]
    rows = []
    for n in range(RING + 1):
        room = 2 if n < RING else 4 * ROWS * ROWS
        for w in list(wanted):
            open_at = max(done[w[1]], *(ready.get((w[0], q), 0) for q in range(w[2], w[2] + w[3])))
            if open_at <= n and w[3] <= room:
                rows.append((n,) + w)
                wanted.remove(w)
                room -= w[3]
    units = []
    for u in range(UNITS - 2, UNITS):
        units.append((max(u, 16), u, 0))
        for way, seq in enumerate(ALONG_Z):
            units += [
                (max(q, 16), u, (NZ - d - 1 if way == 0 else d + 1) % NZ)
                for q, (v, d) in enumerate(seq)
                if v == u
            ]
    return starts, rows, sorted(units, key=lambda e: e[0])


STARTS, ROW_PRODUCTS, UNIT_PRODUCTS = schedule()
STEPS = RING + 1


def lookup(n, values):
    found = jnp.int32(0)
    for at, value in values:
        found = found + jnp.where(n == at, value, 0)
    return found


def before(n, steps):
    count = jnp.int32(0)
    for at in steps:
        count = count + jnp.where(n > at, 1, 0)
    return count


def spread(block, head, rows, write):
    step = 64
    hits = [
        [jnp.broadcast_to(head(s), (step, ORDER)) == float(k) for s in range(STORED)]
        for k in range(SLOTS)
    ]
    for r in range(0, rows, step):
        blocks = [block(s, pl.ds(r, step)) for s in range(STORED)]
        for k in range(SLOTS):
            total = jnp.where(hits[k][0], blocks[0], 0.0)
            for s in range(1, STORED):
                total = total + jnp.where(hits[k][s], blocks[s], 0.0)
            high = total.astype(jnp.bfloat16)
            low = (total - high.astype(jnp.float32)).astype(jnp.bfloat16)
            write(r, step, k, high, low)


def kernel(
    vals, bcols, rcols, out,
    abuf, hdr, stage, bbuf, ad, bhi, blo, cacc, crecv,
    stage_sem, unit_sem, h_send, h_recv, za_send, za_recv, y_send, y_recv, x_send, x_recv, s_send, s_recv, c_send, c_recv,
):
    row, col = lax.axis_index("row"), lax.axis_index("col")
    x, yh, c = lax.div(row, 4), lax.rem(lax.div(row, 2), 2), lax.rem(row, 2)
    z, yl = lax.div(col, 2), lax.rem(col, 2)

    def at_row(x_, yh_, c_):
        return (x_ * 2 + yh_) * 2 + c_

    z_up, z_down = lax.rem(z + 1, NZ), lax.rem(z + NZ - 1, NZ)
    x_up, x_down = lax.rem(x + 1, NX), lax.rem(x + NX - 1, NX)
    sibling = (at_row(x, yh, 1 - c), col)
    partner = (row, z * 2 + 1 - yl)
    z_side = ((row, z_up * 2 + yl), (row, z_down * 2 + yl))
    alone = jnp.logical_and(yh == c, c == yl)

    barrier = pltpu.get_barrier_semaphore()

    def greet(device):
        pl.semaphore_signal(barrier, inc=1, device_id=device, device_id_type=MESH)

    greet(z_side[0])
    greet(z_side[1])
    greet((at_row(x_up, yh, c), col))
    greet((at_row(x_down, yh, c), col))
    greet(sibling)
    greet(partner)
    for k in range(2):
        @pl.when(jnp.logical_not(jnp.logical_and(alone, yh == k)))
        def _():
            greet((at_row(x, k, yh), z * 2 + c))
            greet((at_row(x, c, yl), z * 2 + k))

    def unit_load(u, s):
        p, part = lax.div(u, 2), lax.rem(u, 2)
        rows = pl.ds(pl.multiple_of(s * ORDER + part * HALF, HALF), HALF)
        return pltpu.make_async_copy(
            vals.at[p, rows], abuf.at[z, u, s], unit_sem.at[u, s]
        )

    def row_load(p):
        return pltpu.make_async_copy(
            vals.at[p], stage.at[p, pl.ds(0, BODY)], stage_sem.at[p]
        )

    @pl.loop(0, UNITS)
    def _(u):
        for s in range(STORED):
            unit_load(u, s).start()

    @pl.loop(0, ROWS)
    def _(p):
        row_load(p).start()

    for p in range(ROWS):
        for s in range(8):
            name = bcols[s, 0, p].astype(jnp.float32) if s < STORED else jnp.float32(0)
            line = jnp.full((1, ORDER), name)
            if s < 4:
                hdr[z, p * 4 + s : p * 4 + s + 1, :] = line
            stage[p, BODY + s : BODY + s + 1, :] = line

    @pl.loop(0, 2 * ROWS)
    def _(at):
        cacc[at] = jnp.zeros((ORDER, SLOTS * ORDER), jnp.float32)

    @pl.loop(0, UNITS)
    def _(u):
        for s in range(STORED):
            unit_load(u, s).wait()

    @pl.loop(0, ROWS)
    def _(p):
        row_load(p).wait()

    pl.semaphore_wait(barrier, jnp.where(alone, 8, 10))

    def behind(way, far):
        return lax.rem(z + (NZ - far if way == 0 else far), NZ)

    def z_copy(way, u, d, back):
        ref = abuf.at[behind(way, d + back), u]
        return pltpu.make_async_remote_copy(
            src_ref=ref,
            dst_ref=ref,
            send_sem=za_send.at[way, u * 4 + d],
            recv_sem=za_recv.at[way, u * 4 + d],
            device_id=z_side[way],
            device_id_type=MESH,
        )

    def h_copy(way, d, back):
        ref = hdr.at[behind(way, d + back)]
        return pltpu.make_async_remote_copy(
            src_ref=ref,
            dst_ref=ref,
            send_sem=h_send.at[way, d],
            recv_sem=h_recv.at[way, d],
            device_id=z_side[way],
            device_id_type=MESH,
        )

    turn = 1 - 2 * c

    def along_x(steps):
        return lax.rem(x + steps + 4 * NX, NX)

    def x_copy(k, back):
        i = lax.div(k, PHASE) * ROWS + lax.rem(k, ROWS)
        far = lax.div(lax.rem(k, PHASE), ROWS) + back
        ref = bbuf.at[i, along_x(-turn * far) * 2 + c]
        return pltpu.make_async_remote_copy(
            src_ref=ref,
            dst_ref=ref,
            send_sem=x_send.at[k],
            recv_sem=x_recv.at[k],
            device_id=(at_row(along_x(turn), yh, c), col),
            device_id_type=MESH,
        )

    def s_copy(far, i, back):
        slot = along_x(turn * far) * 2 + 1 - c if back else along_x(-turn * far) * 2 + c
        ref = bbuf.at[i, slot]
        return pltpu.make_async_remote_copy(
            src_ref=ref,
            dst_ref=ref,
            send_sem=s_send.at[far, i],
            recv_sem=s_recv.at[far, i],
            device_id=sibling,
            device_id_type=MESH,
        )

    def y_copy(k, p):
        i = jnp.where(c == yl, ROWS, 0) + p
        return pltpu.make_async_remote_copy(
            src_ref=stage.at[p],
            dst_ref=bbuf.at[i, x * 2 + yh],
            send_sem=y_send.at[k, p],
            recv_sem=y_recv.at[i],
            device_id=(at_row(x, k, yh), z * 2 + c),
            device_id_type=MESH,
        )

    def y_local(p):
        return pltpu.make_async_copy(
            stage.at[p], bbuf.at[ROWS + p, x * 2 + yh], y_recv.at[ROWS + p]
        )

    def y_start():
        @pl.loop(0, ROWS)
        def _(p):
            for k in range(2):
                here = jnp.logical_and(alone, yh == k)
                pl.when(here)(lambda: y_local(p).start())
                pl.when(jnp.logical_not(here))(lambda: y_copy(k, p).start())

    def y_arrive(i):
        ref = bbuf.at[i, x * 2 + c]
        own = jnp.logical_and(alone, i >= ROWS)

        @pl.when(own)
        def _():
            y_local(lax.rem(i, ROWS)).wait()

        @pl.when(jnp.logical_not(own))
        def _():
            pltpu.make_async_remote_copy(
                src_ref=ref,
                dst_ref=ref,
                send_sem=y_send.at[0, 0],
                recv_sem=y_recv.at[i],
                device_id=sibling,
                device_id_type=MESH,
            ).wait_recv()

    def half_row(u):
        return pl.ds(pl.multiple_of(lax.rem(u, 2) * HALF, HALF), HALF)

    def c_copy(u):
        return pltpu.make_async_remote_copy(
            src_ref=cacc.at[lax.div(u, 2), half_row(u)],
            dst_ref=crecv.at[lax.div(u, 2), half_row(u)],
            send_sem=c_send.at[u],
            recv_sem=c_recv.at[u],
            device_id=partner,
            device_id_type=MESH,
        )

    def left_slot(source):
        mine = lax.rem(source, 2) == c
        far = along_x(jnp.where(mine, turn, -turn) * (x - lax.div(source, 2)) - x)
        return far * 2 + jnp.where(mine, 0, 1)

    def in_half(slot):
        return pl.multiple_of(lax.rem(slot, 4) * SLOTS * ORDER, SLOTS * ORDER)

    def spread_left(u, source):
        p, part = lax.div(u, 2), lax.rem(u, 2)
        high_at = pl.multiple_of(HALF + part * HALF, HALF)
        low_at = pl.multiple_of(part * 3 * HALF, HALF)
        slot = left_slot(source)
        lanes = in_half(slot)
        unit = p * 2 + lax.div(slot, 4)

        def write(r, step, k, high, low):
            cols = pl.ds(lanes + k * ORDER, ORDER)
            ad[unit, pl.ds(high_at + r, step), cols] = high
            ad[unit, pl.ds(low_at + r, step), cols] = low

        spread(
            lambda s, rows: abuf[source, u, s, rows, :],
            lambda s: hdr[source, pl.ds(p * 4 + s, 1), :],
            HALF,
            write,
        )

    def right_slot(far, other):
        return along_x((2 * other - 1) * turn * far) * 2 + jnp.where(other == 1, 1 - c, c)

    def spread_right(i, far, other):
        slot = right_slot(far, other)
        base = pl.multiple_of(in_half(far * 2 + other) + lax.rem(i, ROWS) * ORDER, ORDER)
        unit = lax.div(i, ROWS) * 2 + lax.div(far, 2)

        def write(r, step, k, high, low):
            rows = pl.ds(base + r, step)
            cols = pl.ds(k * ORDER, ORDER)
            bhi[unit, rows, cols] = high
            blo[unit, rows, cols] = low

        spread(
            lambda s, rows: bbuf[i, slot, pl.ds(s * ORDER + rows.start, rows.size), :],
            lambda s: bbuf[i, slot, BODY + s : BODY + s + 1, :],
            ORDER,
            write,
        )

    def dot(left, right):
        return jnp.dot(left, right, preferred_element_type=jnp.float32)

    def row_product(phase, p, half, inner):
        both = dot(ad[p * 2 + half, :, inner], bhi[phase * 2 + half, inner, :])
        rest = dot(ad[p * 2 + half, HALF : 3 * HALF, inner], blo[phase * 2 + half, inner, :])
        at = phase * ROWS + p
        cacc[at, 0:HALF, :] += both[0:HALF] + both[HALF : 2 * HALF] + rest[0:HALF]
        cacc[at, HALF:ORDER, :] += (
            both[2 * HALF : 3 * HALF] + both[3 * HALF :] + rest[HALF:]
        )

    def unit_product(u, source):
        p, part = lax.div(u, 2), lax.rem(u, 2)
        whole = pl.ds(pl.multiple_of(part * ORDER, ORDER), ORDER)
        highs = pl.ds(pl.multiple_of(HALF + part * HALF, HALF), HALF)
        slot = left_slot(source)
        inner = pl.ds(in_half(slot), SLOTS * ORDER)
        half = lax.div(slot, 4)
        both = dot(ad[p * 2 + half, whole, inner], bhi[half, inner, :])
        rest = dot(ad[p * 2 + half, highs, inner], blo[half, inner, :])
        cacc[p, half_row(u), :] += both[0:HALF] + both[HALF:] + rest

    def z_sent(u):
        for way, seq in enumerate(ALONG_Z):
            for d in range(sum(part[0] == u for part in seq)):
                z_copy(way, u, d, 0).wait_send()

    def y_sent(p):
        for k in range(2):
            pl.when(jnp.logical_not(jnp.logical_and(alone, yh == k)))(
                lambda: y_copy(k, p).wait_send()
            )

    def x_sent(k):
        x_copy(k, 0).wait_send()
        i = lax.div(k, PHASE) * ROWS + lax.rem(k, ROWS)
        s_copy(lax.div(lax.rem(k, PHASE), ROWS) + 1, i, 0).wait_send()

    for way in range(2):
        h_copy(way, 0, 0).start()
    for way in range(2):
        for at, u in STARTS[way]:
            if at < 0:
                z_copy(way, u, 0, 0).start()

    @pl.loop(0, STEPS)
    def _(n):
        arrived = [
            lookup(n, [(q, u * 4 + d) for q, (u, d) in enumerate(seq)]) for seq in ALONG_Z
        ]

        @pl.when(n == jnp.where(c == yl, 4, 0))
        def _():
            y_start()

        @pl.when(jnp.logical_or(n < ROWS, jnp.logical_and(n >= 10, n < 10 + ROWS)))
        def _():
            i = jnp.where(n < ROWS, n, n - 10 + ROWS)
            y_arrive(i)
            x_copy(lax.div(i, ROWS) * PHASE + lax.rem(i, ROWS), 0).start()
            s_copy(0, i, 0).start()

        for d in range(4):
            @pl.when(n == (0, 2, 5, 8)[d])
            def _():
                for way in range(2):
                    if d < HEAD_HOPS[way]:
                        h_copy(way, d, 1).wait_recv()
                    if d + 1 < HEAD_HOPS[way]:
                        h_copy(way, d + 1, 0).start()

        @pl.when(n < RING)
        def _():
            for way in range(2):
                u, d = lax.div(arrived[way], 4), lax.rem(arrived[way], 4)
                z_copy(way, u, d, 1).wait_recv()
                last = lookup(
                    u, [(v, sum(part[0] == v for part in ALONG_Z[way]) - 1) for v in range(UNITS)]
                )

                @pl.when(d < last)
                def _():
                    z_copy(way, u, d + 1, 0).start()

                steps = [at for at, _ in STARTS[way]]

                @pl.loop(before(n, steps), before(n + 1, steps))
                def _(j):
                    own = lookup(j, [(e, v) for e, (_, v) in enumerate(STARTS[way])])
                    z_copy(way, own, 0, 0).start()

        k = n - 2

        @pl.when(jnp.logical_and(k >= 0, k < 2 * PHASE))
        def _():
            x_copy(k, 1).wait_recv()

            @pl.when(lax.rem(k, PHASE) < 2 * ROWS)
            def _():
                x_copy(k + ROWS, 0).start()

            i = lax.div(k, PHASE) * ROWS + lax.rem(k, ROWS)
            s_copy(lax.div(lax.rem(k, PHASE), ROWS) + 1, i, 0).start()

        @pl.loop(jnp.where(n < RING, 0, 3), jnp.where(n < UNITS, 3, jnp.where(n < RING, 2, 3)))
        def _(j):
            part = jnp.where(j == 0, arrived[0], jnp.where(j == 1, arrived[1], n * 4))
            far = lax.rem(part, 4) + 1
            away = jnp.where(j == 0, NZ - far, jnp.where(j == 1, far, 0))
            spread_left(lax.div(part, 4), lax.rem(z + away, NZ))

        steps = [at for at, _, _ in UNIT_PRODUCTS]

        @pl.loop(before(n, steps), before(n + 1, steps))
        def _(j):
            code = lookup(j, [(e, u * NZ + a) for e, (_, u, a) in enumerate(UNIT_PRODUCTS)])
            unit_product(lax.div(code, NZ), lax.rem(z + lax.rem(code, NZ), NZ))

        for u in range(UNITS - 2, UNITS):
            @pl.when(n == max(at for at, v, _ in UNIT_PRODUCTS if v == u))
            def _():
                c_copy(u).start()

        def both_cores(far, i):
            s_copy(far, i, 1).wait_recv()

            @pl.loop(0, 2)
            def _(other):
                spread_right(i, far, other)

        own = jnp.logical_or(
            jnp.logical_and(n >= 1, n < 1 + ROWS), jnp.logical_and(n >= 11, n < 11 + ROWS)
        )
        came = jnp.logical_and(n >= 3, n < 3 + 2 * PHASE)
        k_came = jnp.clip(n - 3, 0, 2 * PHASE - 1)
        i_own = jnp.where(n < 1 + ROWS, jnp.maximum(n - 1, 0), n - 11 + ROWS)
        i_came = lax.div(k_came, PHASE) * ROWS + lax.rem(k_came, ROWS)

        @pl.loop(jnp.where(own, 0, 1), jnp.where(came, 2, 1))
        def _(j):
            both_cores(
                jnp.where(j == 0, 0, lax.div(lax.rem(k_came, PHASE), ROWS) + 1),
                jnp.where(j == 0, i_own, i_came),
            )

        for u in range(UNITS - 2):
            @pl.when(n == 20 + u)
            def _():
                z_sent(u)

        @pl.when(jnp.logical_and(n >= 6, n < 6 + EARLY))
        def _():
            x_sent(n - 6)

        @pl.when(jnp.logical_and(n >= 18, n < 18 + 2 * ROWS))
        def _():
            s_copy(0, n - 18, 0).wait_send()

        @pl.when(jnp.logical_and(n >= 16, n < 16 + ROWS))
        def _():
            y_sent(n - 16)

        @pl.when(n == 15)
        def _():
            for way in range(2):
                for d in range(HEAD_HOPS[way]):
                    h_copy(way, d, 0).wait_send()

        row_steps = [e[0] for e in ROW_PRODUCTS]

        @pl.loop(before(n, row_steps), before(n + 1, row_steps))
        def _(j):
            code = lookup(
                j,
                [
                    (e, ((phase * ROWS + p) * 4 + q) * 2 + count - 1)
                    for e, (_, phase, p, q, count) in enumerate(ROW_PRODUCTS)
                ],
            )
            row, quarter = lax.div(code, 8), lax.rem(lax.div(code, 2), 4)
            phase, p, half = lax.div(row, ROWS), lax.rem(row, ROWS), lax.div(quarter, 2)
            depth = 2 * SLOTS * ORDER

            @pl.when(lax.rem(code, 2) == 1)
            def _():
                row_product(phase, p, half, pl.ds(0, 2 * depth))

            @pl.when(lax.rem(code, 2) == 0)
            def _():
                start = pl.multiple_of(lax.rem(quarter, 2) * depth, depth)
                row_product(phase, p, half, pl.ds(start, depth))

            @pl.when(jnp.logical_and(phase == 0, half == 1))
            def _():
                c_copy(p * 2).start()
                c_copy(p * 2 + 1).start()

    for u in range(UNITS - 2, UNITS):
        z_sent(u)

    @pl.loop(EARLY, 2 * PHASE)
    def _(k):
        x_sent(k)

    @pl.loop(0, ROWS)
    def _(p):
        c_copy(p * 2).wait_recv()
        c_copy(p * 2 + 1).wait_recv()
        wants = [rcols[p, 0, u] for u in range(SLOTS)]
        for r in range(0, ORDER, 32):
            rows = slice(r, r + 32)
            both = [
                cacc[ROWS + p, rows, k * ORDER : (k + 1) * ORDER]
                + crecv[p, rows, k * ORDER : (k + 1) * ORDER]
                for k in range(SLOTS)
            ]
            for u in range(SLOTS):
                block = both[0]
                for k in range(1, SLOTS):
                    block = jnp.where(wants[u] == k, both[k], block)
                out[p, 0, u, rows, :] = block

    @pl.loop(0, UNITS)
    def _(u):
        c_copy(u).wait_send()


def on_device(block_values, block_cols, result_cols):
    vals = block_values.reshape(ROWS, BODY, ORDER)
    dma = pltpu.SemaphoreType.DMA
    return pl.pallas_call(
        kernel,
        out_shape=pltpu.VMEM((ROWS, 1, SLOTS, ORDER, ORDER), jnp.float32),
        in_specs=[
            pl.BlockSpec(memory_space=pl.ANY),
            pl.BlockSpec(memory_space=pltpu.SMEM),
            pl.BlockSpec(memory_space=pltpu.SMEM),
        ],
        out_specs=pl.BlockSpec(memory_space=pltpu.VMEM),
        scratch_shapes=[
            pltpu.VMEM((NZ, UNITS, STORED, HALF, ORDER), jnp.float32),
            pltpu.VMEM((NZ, 4 * ROWS, ORDER), jnp.float32),
            pltpu.VMEM((ROWS, PIECE, ORDER), jnp.float32),
            pltpu.VMEM((2 * ROWS, 2 * NX, PIECE, ORDER), jnp.float32),
            pltpu.VMEM((2 * ROWS, 2 * ORDER, 4 * SLOTS * ORDER), jnp.bfloat16),
            pltpu.VMEM((4, 4 * SLOTS * ORDER, SLOTS * ORDER), jnp.bfloat16),
            pltpu.VMEM((4, 4 * SLOTS * ORDER, SLOTS * ORDER), jnp.bfloat16),
            pltpu.VMEM((2 * ROWS, ORDER, SLOTS * ORDER), jnp.float32),
            pltpu.VMEM((ROWS, ORDER, SLOTS * ORDER), jnp.float32),
            dma((ROWS,)),
            dma((UNITS, STORED)),
            dma((2, 4)),
            dma((2, 4)),
            dma((2, 4 * UNITS)),
            dma((2, 4 * UNITS)),
            dma((2, ROWS)),
            dma((2 * ROWS,)),
            dma((2 * PHASE,)),
            dma((2 * PHASE,)),
            dma((4, 2 * ROWS)),
            dma((4, 2 * ROWS)),
            dma((UNITS,)),
            dma((UNITS,)),
        ],
        compiler_params=pltpu.CompilerParams(
            collective_id=0, has_side_effects=True, vmem_limit_bytes=60 * 2**20
        ),
    )(vals, jnp.transpose(block_cols, (2, 1, 0)), result_cols)


def solution(mesh):
    return jax.shard_map(
        on_device,
        mesh=mesh,
        in_specs=(P("row", "col", None, None, None), P("row", "col", None), P("row", "col", None)),
        out_specs=P("row", "col", None, None, None),
        check_vma=False,
    )
```

```python
import functools

import jax
import jax.numpy as jnp
from jax import lax
from jax.experimental import pallas as pl
from jax.experimental.pallas import tpu as pltpu
from jax.sharding import PartitionSpec as P

MESH = pl.DeviceIdType.MESH
NX, NZ = 4, 8
ORDER = 128
STORED, SLOTS, ROWS = 3, 4, 4
BODY = STORED * ORDER
PIECE = BODY + 8
UNITS = 2 * ROWS
HALF = ORDER // 2
PHASE = 3 * ROWS
EARLY = 22

ALONG_Z = (
    (
        (0, 0), (1, 0), (0, 1), (1, 1), (2, 0), (0, 2), (3, 0),
        (1, 2), (0, 3), (2, 1), (3, 1), (4, 0), (2, 2), (5, 0),
        (3, 2), (2, 3), (4, 1), (5, 1), (6, 0), (4, 2), (5, 2),
        (6, 1), (4, 3), (7, 0), (6, 2), (7, 1), (6, 3), (7, 2),
    ),
    (
        (1, 0), (0, 0), (1, 1), (0, 1), (3, 0), (1, 2), (2, 0),
        (0, 2), (1, 3), (3, 1), (2, 1), (5, 0), (3, 2), (4, 0),
        (2, 2), (3, 3), (5, 1), (4, 1), (7, 0), (5, 2), (6, 0),
        (4, 2), (5, 3), (7, 1), (6, 1), (7, 2), (6, 2), (7, 3),
    ),
)
RING = len(ALONG_Z[0])
HEAD_HOPS = (4, 3)


def schedule():
    starts = []
    for seq in ALONG_Z:
        at = {part: q for q, part in enumerate(seq)}
        issue, own = -1, []
        for q, (u, d) in enumerate(seq):
            if d > 0:
                issue = at[(u, d - 1)]
            else:
                own.append((issue, u))
        starts.append(sorted(own, key=lambda e: e[0]))
    done = [max(q for seq in ALONG_Z for q, (v, _) in enumerate(seq) if v == u) for u in range(UNITS)]
    done = [max(done[2 * p : 2 * p + 2]) for p in range(ROWS)]
    ready = {(0, 0): 6, (0, 2): 14, (1, 0): 18, (1, 2): 22, (1, 3): 26}
    wanted = [(0, p, q, 2) for p in range(ROWS - 1) for q in (0, 2)]
    wanted += [(1, p, 0, 2) for p in range(ROWS - 1)]
    wanted += [(1, p, q, 1) for q in (2, 3) for p in range(ROWS - 1)]
    wanted += [(1, ROWS - 1, q, 2) for q in (0, 2)]
    rows = []
    for n in range(RING + 1):
        room = (0 if n == RING - 2 else 2) if n < RING else 4 * ROWS * ROWS
        for w in list(wanted):
            open_at = max(done[w[1]], *(ready.get((w[0], q), 0) for q in range(w[2], w[2] + w[3])))
            if open_at <= n and w[3] <= room:
                rows.append((n,) + w)
                wanted.remove(w)
                room -= w[3]
    units = []
    for u in range(UNITS - 2, UNITS):
        units.append((max(u, 16), u, 0))
        for way, seq in enumerate(ALONG_Z):
            units += [
                (max(q, 16), u, (NZ - d - 1 if way == 0 else d + 1) % NZ)
                for q, (v, d) in enumerate(seq)
                if v == u
            ]
    return starts, rows, sorted(units, key=lambda e: e[0])


STARTS, ROW_PRODUCTS, UNIT_PRODUCTS = schedule()
STEPS = RING + 1


def lookup(n, values):
    found = jnp.int32(0)
    for at, value in values:
        found = found + jnp.where(n == at, value, 0)
    return found


def before(n, steps):
    count = jnp.int32(0)
    for at in steps:
        count = count + jnp.where(n > at, 1, 0)
    return count


def spread(block, head, rows, write):
    step = 64
    hits = [
        [jnp.broadcast_to(head(s), (step, ORDER)) == float(k) for s in range(STORED)]
        for k in range(SLOTS)
    ]
    for r in range(0, rows, step):
        blocks = [block(s, pl.ds(r, step)) for s in range(STORED)]
        for k in range(SLOTS):
            total = jnp.where(hits[k][0], blocks[0], 0.0)
            for s in range(1, STORED):
                total = total + jnp.where(hits[k][s], blocks[s], 0.0)
            high = total.astype(jnp.bfloat16)
            low = (total - high.astype(jnp.float32)).astype(jnp.bfloat16)
            write(r, step, k, high, low)


def kernel(
    vals, bcols, rcols, out,
    abuf, hdr, stage, bbuf, ad, bhi, blo, cacc, crecv,
    stage_sem, unit_sem, h_send, h_recv, za_send, za_recv, y_send, y_recv, x_send, x_recv, s_send, s_recv, c_send, c_recv,
):
    row, col = lax.axis_index("row"), lax.axis_index("col")
    x, yh, c = lax.div(row, 4), lax.rem(lax.div(row, 2), 2), lax.rem(row, 2)
    z, yl = lax.div(col, 2), lax.rem(col, 2)

    def at_row(x_, yh_, c_):
        return (x_ * 2 + yh_) * 2 + c_

    z_up, z_down = lax.rem(z + 1, NZ), lax.rem(z + NZ - 1, NZ)
    x_up, x_down = lax.rem(x + 1, NX), lax.rem(x + NX - 1, NX)
    sibling = (at_row(x, yh, 1 - c), col)
    partner = (row, z * 2 + 1 - yl)
    z_side = ((row, z_up * 2 + yl), (row, z_down * 2 + yl))
    alone = jnp.logical_and(yh == c, c == yl)

    def unit_load(u, s):
        p, part = lax.div(u, 2), lax.rem(u, 2)
        rows = pl.ds(pl.multiple_of(s * ORDER + part * HALF, HALF), HALF)
        return pltpu.make_async_copy(
            vals.at[p, rows], abuf.at[z, u, s], unit_sem.at[u, s]
        )

    def row_load(p):
        return pltpu.make_async_copy(
            vals.at[p], stage.at[p, pl.ds(0, BODY)], stage_sem.at[p]
        )

    @pl.loop(0, UNITS)
    def _(u):
        for s in range(STORED):
            unit_load(u, s).start()

    @pl.loop(0, ROWS)
    def _(p):
        row_load(p).start()

    barrier = pltpu.get_barrier_semaphore()

    def greet(device):
        pl.semaphore_signal(barrier, inc=1, device_id=device, device_id_type=MESH)

    greet(z_side[0])
    greet(z_side[1])
    greet((at_row(x_up, yh, c), col))
    greet((at_row(x_down, yh, c), col))
    greet(sibling)
    greet(partner)
    for k in range(2):
        @pl.when(jnp.logical_not(jnp.logical_and(alone, yh == k)))
        def _():
            greet((at_row(x, k, yh), z * 2 + c))
            greet((at_row(x, c, yl), z * 2 + k))

    for p in range(ROWS):
        for s in range(8):
            name = bcols[s, 0, p].astype(jnp.float32) if s < STORED else jnp.float32(0)
            line = jnp.full((1, ORDER), name)
            if s < 4:
                hdr[z, p * 4 + s : p * 4 + s + 1, :] = line
            stage[p, BODY + s : BODY + s + 1, :] = line

    @pl.loop(0, 2 * ROWS)
    def _(at):
        cacc[at] = jnp.zeros((ORDER, SLOTS * ORDER), jnp.float32)

    @pl.loop(0, UNITS)
    def _(u):
        for s in range(STORED):
            unit_load(u, s).wait()

    @pl.loop(0, ROWS)
    def _(p):
        row_load(p).wait()

    pl.semaphore_wait(barrier, jnp.where(alone, 8, 10))

    def behind(way, far):
        return lax.rem(z + (NZ - far if way == 0 else far), NZ)

    def z_copy(way, u, d, back):
        ref = abuf.at[behind(way, d + back), u]
        return pltpu.make_async_remote_copy(
            src_ref=ref,
            dst_ref=ref,
            send_sem=za_send.at[way, u * 4 + d],
            recv_sem=za_recv.at[way, u * 4 + d],
            device_id=z_side[way],
            device_id_type=MESH,
        )

    def h_copy(way, d, back):
        ref = hdr.at[behind(way, d + back)]
        return pltpu.make_async_remote_copy(
            src_ref=ref,
            dst_ref=ref,
            send_sem=h_send.at[way, d],
            recv_sem=h_recv.at[way, d],
            device_id=z_side[way],
            device_id_type=MESH,
        )

    turn = 1 - 2 * c

    def along_x(steps):
        return lax.rem(x + steps + 4 * NX, NX)

    def x_copy(k, back):
        i = lax.div(k, PHASE) * ROWS + lax.rem(k, ROWS)
        far = lax.div(lax.rem(k, PHASE), ROWS) + back
        ref = bbuf.at[i, along_x(-turn * far) * 2 + c]
        return pltpu.make_async_remote_copy(
            src_ref=ref,
            dst_ref=ref,
            send_sem=x_send.at[k],
            recv_sem=x_recv.at[k],
            device_id=(at_row(along_x(turn), yh, c), col),
            device_id_type=MESH,
        )

    def s_copy(far, i, back):
        slot = along_x(turn * far) * 2 + 1 - c if back else along_x(-turn * far) * 2 + c
        ref = bbuf.at[i, slot]
        return pltpu.make_async_remote_copy(
            src_ref=ref,
            dst_ref=ref,
            send_sem=s_send.at[far, i],
            recv_sem=s_recv.at[far, i],
            device_id=sibling,
            device_id_type=MESH,
        )

    def y_copy(k, p):
        i = jnp.where(c == yl, ROWS, 0) + p
        return pltpu.make_async_remote_copy(
            src_ref=stage.at[p],
            dst_ref=bbuf.at[i, x * 2 + yh],
            send_sem=y_send.at[k, p],
            recv_sem=y_recv.at[i],
            device_id=(at_row(x, k, yh), z * 2 + c),
            device_id_type=MESH,
        )

    def y_local(p):
        return pltpu.make_async_copy(
            stage.at[p], bbuf.at[ROWS + p, x * 2 + yh], y_recv.at[ROWS + p]
        )

    def y_start():
        @pl.loop(0, ROWS)
        def _(p):
            for k in range(2):
                here = jnp.logical_and(alone, yh == k)
                pl.when(here)(lambda: y_local(p).start())
                pl.when(jnp.logical_not(here))(lambda: y_copy(k, p).start())

    def y_arrive(i):
        ref = bbuf.at[i, x * 2 + c]
        own = jnp.logical_and(alone, i >= ROWS)

        @pl.when(own)
        def _():
            y_local(lax.rem(i, ROWS)).wait()

        @pl.when(jnp.logical_not(own))
        def _():
            pltpu.make_async_remote_copy(
                src_ref=ref,
                dst_ref=ref,
                send_sem=y_send.at[0, 0],
                recv_sem=y_recv.at[i],
                device_id=sibling,
                device_id_type=MESH,
            ).wait_recv()

    def half_row(u):
        return pl.ds(pl.multiple_of(lax.rem(u, 2) * HALF, HALF), HALF)

    def c_copy(u):
        return pltpu.make_async_remote_copy(
            src_ref=cacc.at[lax.div(u, 2), half_row(u)],
            dst_ref=crecv.at[lax.div(u, 2), half_row(u)],
            send_sem=c_send.at[u],
            recv_sem=c_recv.at[u],
            device_id=partner,
            device_id_type=MESH,
        )

    def left_slot(source):
        mine = lax.rem(source, 2) == c
        far = along_x(jnp.where(mine, turn, -turn) * (x - lax.div(source, 2)) - x)
        return far * 2 + jnp.where(mine, 0, 1)

    def in_half(slot):
        return pl.multiple_of(lax.rem(slot, 4) * SLOTS * ORDER, SLOTS * ORDER)

    def spread_left(u, source):
        p, part = lax.div(u, 2), lax.rem(u, 2)
        high_at = pl.multiple_of(HALF + part * HALF, HALF)
        low_at = pl.multiple_of(part * 3 * HALF, HALF)
        slot = left_slot(source)
        lanes = in_half(slot)
        unit = p * 2 + lax.div(slot, 4)

        def write(r, step, k, high, low):
            cols = pl.ds(lanes + k * ORDER, ORDER)
            ad[unit, pl.ds(high_at + r, step), cols] = high
            ad[unit, pl.ds(low_at + r, step), cols] = low

        spread(
            lambda s, rows: abuf[source, u, s, rows, :],
            lambda s: hdr[source, pl.ds(p * 4 + s, 1), :],
            HALF,
            write,
        )

    def right_slot(far, other):
        return along_x((2 * other - 1) * turn * far) * 2 + jnp.where(other == 1, 1 - c, c)

    def spread_right(i, far, other):
        slot = right_slot(far, other)
        base = pl.multiple_of(in_half(far * 2 + other) + lax.rem(i, ROWS) * ORDER, ORDER)
        unit = lax.div(i, ROWS) * 2 + lax.div(far, 2)

        def write(r, step, k, high, low):
            rows = pl.ds(base + r, step)
            cols = pl.ds(k * ORDER, ORDER)
            bhi[unit, rows, cols] = high
            blo[unit, rows, cols] = low

        spread(
            lambda s, rows: bbuf[i, slot, pl.ds(s * ORDER + rows.start, rows.size), :],
            lambda s: bbuf[i, slot, BODY + s : BODY + s + 1, :],
            ORDER,
            write,
        )

    def dot(left, right):
        return jnp.dot(left, right, preferred_element_type=jnp.float32)

    def row_product(phase, p, half, inner):
        both = dot(ad[p * 2 + half, :, inner], bhi[phase * 2 + half, inner, :])
        rest = dot(ad[p * 2 + half, HALF : 3 * HALF, inner], blo[phase * 2 + half, inner, :])
        at = phase * ROWS + p
        cacc[at, 0:HALF, :] += both[0:HALF] + both[HALF : 2 * HALF] + rest[0:HALF]
        cacc[at, HALF:ORDER, :] += (
            both[2 * HALF : 3 * HALF] + both[3 * HALF :] + rest[HALF:]
        )

    def unit_product(u, source):
        p, part = lax.div(u, 2), lax.rem(u, 2)
        whole = pl.ds(pl.multiple_of(part * ORDER, ORDER), ORDER)
        highs = pl.ds(pl.multiple_of(HALF + part * HALF, HALF), HALF)
        slot = left_slot(source)
        inner = pl.ds(in_half(slot), SLOTS * ORDER)
        half = lax.div(slot, 4)
        both = dot(ad[p * 2 + half, whole, inner], bhi[half, inner, :])
        rest = dot(ad[p * 2 + half, highs, inner], blo[half, inner, :])
        cacc[p, half_row(u), :] += both[0:HALF] + both[HALF:] + rest

    def z_sent(u):
        for way, seq in enumerate(ALONG_Z):
            for d in range(sum(part[0] == u for part in seq)):
                z_copy(way, u, d, 0).wait_send()

    def y_sent(p):
        for k in range(2):
            pl.when(jnp.logical_not(jnp.logical_and(alone, yh == k)))(
                lambda: y_copy(k, p).wait_send()
            )

    def x_sent(k):
        x_copy(k, 0).wait_send()
        i = lax.div(k, PHASE) * ROWS + lax.rem(k, ROWS)
        s_copy(lax.div(lax.rem(k, PHASE), ROWS) + 1, i, 0).wait_send()

    for way in range(2):
        h_copy(way, 0, 0).start()
    for way in range(2):
        for at, u in STARTS[way]:
            if at < 0:
                z_copy(way, u, 0, 0).start()

    @pl.loop(0, STEPS)
    def _(n):
        arrived = [
            lookup(n, [(q, u * 4 + d) for q, (u, d) in enumerate(seq)]) for seq in ALONG_Z
        ]

        @pl.when(n == jnp.where(c == yl, 4, 0))
        def _():
            y_start()

        @pl.when(jnp.logical_or(n < ROWS, jnp.logical_and(n >= 10, n < 10 + ROWS)))
        def _():
            i = jnp.where(n < ROWS, n, n - 10 + ROWS)
            y_arrive(i)
            x_copy(lax.div(i, ROWS) * PHASE + lax.rem(i, ROWS), 0).start()
            s_copy(0, i, 0).start()

        for d in range(4):
            @pl.when(n == (0, 2, 5, 8)[d])
            def _():
                for way in range(2):
                    if d < HEAD_HOPS[way]:
                        h_copy(way, d, 1).wait_recv()
                    if d + 1 < HEAD_HOPS[way]:
                        h_copy(way, d + 1, 0).start()

        @pl.when(n < RING)
        def _():
            for way in range(2):
                u, d = lax.div(arrived[way], 4), lax.rem(arrived[way], 4)
                z_copy(way, u, d, 1).wait_recv()
                last = lookup(
                    u, [(v, sum(part[0] == v for part in ALONG_Z[way]) - 1) for v in range(UNITS)]
                )

                @pl.when(d < last)
                def _():
                    z_copy(way, u, d + 1, 0).start()

                steps = [at for at, _ in STARTS[way]]

                @pl.loop(before(n, steps), before(n + 1, steps))
                def _(j):
                    own = lookup(j, [(e, v) for e, (_, v) in enumerate(STARTS[way])])
                    z_copy(way, own, 0, 0).start()

        k = n - 2

        @pl.when(jnp.logical_and(k >= 0, k < 2 * PHASE))
        def _():
            x_copy(k, 1).wait_recv()

            @pl.when(lax.rem(k, PHASE) < 2 * ROWS)
            def _():
                x_copy(k + ROWS, 0).start()

            i = lax.div(k, PHASE) * ROWS + lax.rem(k, ROWS)
            s_copy(lax.div(lax.rem(k, PHASE), ROWS) + 1, i, 0).start()

        @pl.loop(jnp.where(n < RING, 0, 3), jnp.where(n < UNITS, 3, jnp.where(n < RING, 2, 3)))
        def _(j):
            part = jnp.where(j == 0, arrived[0], jnp.where(j == 1, arrived[1], n * 4))
            far = lax.rem(part, 4) + 1
            away = jnp.where(j == 0, NZ - far, jnp.where(j == 1, far, 0))
            spread_left(lax.div(part, 4), lax.rem(z + away, NZ))

        steps = [at for at, _, _ in UNIT_PRODUCTS]

        @pl.loop(before(n, steps), before(n + 1, steps))
        def _(j):
            code = lookup(j, [(e, u * NZ + a) for e, (_, u, a) in enumerate(UNIT_PRODUCTS)])
            unit_product(lax.div(code, NZ), lax.rem(z + lax.rem(code, NZ), NZ))

        for u in range(UNITS - 2, UNITS):
            @pl.when(n == max(at for at, v, _ in UNIT_PRODUCTS if v == u))
            def _():
                c_copy(u).start()

        def both_cores(far, i):
            s_copy(far, i, 1).wait_recv()

            @pl.loop(0, 2)
            def _(other):
                spread_right(i, far, other)

        own = jnp.logical_or(
            jnp.logical_and(n >= 1, n < 1 + ROWS), jnp.logical_and(n >= 11, n < 11 + ROWS)
        )
        came = jnp.logical_and(n >= 3, n < 3 + 2 * PHASE)
        k_came = jnp.clip(n - 3, 0, 2 * PHASE - 1)
        i_own = jnp.where(n < 1 + ROWS, jnp.maximum(n - 1, 0), n - 11 + ROWS)
        i_came = lax.div(k_came, PHASE) * ROWS + lax.rem(k_came, ROWS)

        @pl.loop(jnp.where(own, 0, 1), jnp.where(came, 2, 1))
        def _(j):
            both_cores(
                jnp.where(j == 0, 0, lax.div(lax.rem(k_came, PHASE), ROWS) + 1),
                jnp.where(j == 0, i_own, i_came),
            )

        for u in range(UNITS - 2):
            @pl.when(n == 20 + u)
            def _():
                z_sent(u)

        @pl.when(jnp.logical_and(n >= 6, n < 6 + EARLY))
        def _():
            x_sent(n - 6)

        @pl.when(jnp.logical_and(n >= 18, n < 18 + 2 * ROWS))
        def _():
            s_copy(0, n - 18, 0).wait_send()

        @pl.when(jnp.logical_and(n >= 16, n < 16 + ROWS))
        def _():
            y_sent(n - 16)

        @pl.when(n == 15)
        def _():
            for way in range(2):
                for d in range(HEAD_HOPS[way]):
                    h_copy(way, d, 0).wait_send()

        row_steps = [e[0] for e in ROW_PRODUCTS]

        @pl.loop(before(n, row_steps), before(n + 1, row_steps))
        def _(j):
            code = lookup(
                j,
                [
                    (e, ((phase * ROWS + p) * 4 + q) * 2 + count - 1)
                    for e, (_, phase, p, q, count) in enumerate(ROW_PRODUCTS)
                ],
            )
            row, quarter = lax.div(code, 8), lax.rem(lax.div(code, 2), 4)
            phase, p, half = lax.div(row, ROWS), lax.rem(row, ROWS), lax.div(quarter, 2)
            depth = 2 * SLOTS * ORDER

            @pl.when(lax.rem(code, 2) == 1)
            def _():
                row_product(phase, p, half, pl.ds(0, 2 * depth))

            @pl.when(lax.rem(code, 2) == 0)
            def _():
                start = pl.multiple_of(lax.rem(quarter, 2) * depth, depth)
                row_product(phase, p, half, pl.ds(start, depth))

            @pl.when(jnp.logical_and(phase == 0, half == 1))
            def _():
                c_copy(p * 2).start()
                c_copy(p * 2 + 1).start()

    for u in range(UNITS - 2, UNITS):
        z_sent(u)

    @pl.loop(EARLY, 2 * PHASE)
    def _(k):
        x_sent(k)

    @pl.loop(0, ROWS)
    def _(p):
        c_copy(p * 2).wait_recv()
        c_copy(p * 2 + 1).wait_recv()
        wants = [rcols[p, 0, u] for u in range(SLOTS)]
        for r in range(0, ORDER, 32):
            rows = slice(r, r + 32)
            both = [
                cacc[ROWS + p, rows, k * ORDER : (k + 1) * ORDER]
                + crecv[p, rows, k * ORDER : (k + 1) * ORDER]
                for k in range(SLOTS)
            ]
            for u in range(SLOTS):
                block = both[0]
                for k in range(1, SLOTS):
                    block = jnp.where(wants[u] == k, both[k], block)
                out[p, 0, u, rows, :] = block

    @pl.loop(0, UNITS)
    def _(u):
        c_copy(u).wait_send()


def on_device(block_values, block_cols, result_cols):
    vals = block_values.reshape(ROWS, BODY, ORDER)
    dma = pltpu.SemaphoreType.DMA
    return pl.pallas_call(
        kernel,
        out_shape=pltpu.VMEM((ROWS, 1, SLOTS, ORDER, ORDER), jnp.float32),
        in_specs=[
            pl.BlockSpec(memory_space=pl.ANY),
            pl.BlockSpec(memory_space=pltpu.SMEM),
            pl.BlockSpec(memory_space=pltpu.SMEM),
        ],
        out_specs=pl.BlockSpec(memory_space=pltpu.VMEM),
        scratch_shapes=[
            pltpu.VMEM((NZ, UNITS, STORED, HALF, ORDER), jnp.float32),
            pltpu.VMEM((NZ, 4 * ROWS, ORDER), jnp.float32),
            pltpu.VMEM((ROWS, PIECE, ORDER), jnp.float32),
            pltpu.VMEM((2 * ROWS, 2 * NX, PIECE, ORDER), jnp.float32),
            pltpu.VMEM((2 * ROWS, 2 * ORDER, 4 * SLOTS * ORDER), jnp.bfloat16),
            pltpu.VMEM((4, 4 * SLOTS * ORDER, SLOTS * ORDER), jnp.bfloat16),
            pltpu.VMEM((4, 4 * SLOTS * ORDER, SLOTS * ORDER), jnp.bfloat16),
            pltpu.VMEM((2 * ROWS, ORDER, SLOTS * ORDER), jnp.float32),
            pltpu.VMEM((ROWS, ORDER, SLOTS * ORDER), jnp.float32),
            dma((ROWS,)),
            dma((UNITS, STORED)),
            dma((2, 4)),
            dma((2, 4)),
            dma((2, 4 * UNITS)),
            dma((2, 4 * UNITS)),
            dma((2, ROWS)),
            dma((2 * ROWS,)),
            dma((2 * PHASE,)),
            dma((2 * PHASE,)),
            dma((4, 2 * ROWS)),
            dma((4, 2 * ROWS)),
            dma((UNITS,)),
            dma((UNITS,)),
        ],
        compiler_params=pltpu.CompilerParams(
            collective_id=0, has_side_effects=True, vmem_limit_bytes=60 * 2**20
        ),
    )(vals, jnp.transpose(block_cols, (2, 1, 0)), result_cols)


def solution(mesh):
    return jax.shard_map(
        on_device,
        mesh=mesh,
        in_specs=(P("row", "col", None, None, None), P("row", "col", None), P("row", "col", None)),
        out_specs=P("row", "col", None, None, None),
        check_vma=False,
    )
```
